256 devices in a mesh: context: 16 (over x, y), tensor: 16 (over z, core).
Axes of the slice: x: 4, y: 4, z: 8, core: 2. Of those that a mesh axis runs over, the one named last changes fastest.
Arguments:
- query_rows: bfloat16 [2048, 8192], P('context', 'tensor'), may hold values from -6 to 6
- key_rows: bfloat16 [2048, 8192], P('context', 'tensor'), may hold values from -6 to 6
- value_rows: bfloat16 [2048, 8192], P('context', 'tensor'), may hold values from -6 to 6
- residue: float32 [16, 8192], P(None, 'tensor'), may hold values from -3 to 3
- decay_rate: float32 [16, 8192], P(None, 'tensor'), may hold values from 9.765625e-05 to 0.04
- out_weight: bfloat16 [8192, 8192], P('tensor'), may hold values from -0.09375 to 0.09375
- cotangent: bfloat16 [2048, 8192], P('context', 'tensor'), may hold values from -6 to 6
Outputs:
- mixed_out: bfloat16 [2048, 8192], P('context', 'tensor')
- query_grad: bfloat16 [2048, 8192], P('context', 'tensor')
- key_grad: bfloat16 [2048, 8192], P('context', 'tensor')
- value_grad: bfloat16 [2048, 8192], P('context', 'tensor')
- weight_grad: bfloat16 [8192, 8192], P('tensor', 'context')
The draws below stay inside these ranges and needn't reach their ends.
All inputs are finite; a program needn't handle non-finite values.
Results may differ from the reference program's by a relative error of at most 0.027.
Values may be sent and summed in bfloat16 or wider, within the bound.
A program may use at most 128 MiB of HBM per device.

```python
import math
import jax
import jax.numpy as jnp
from jax import lax

D = 8192
MODES = 16
SEQ = 2048
N_CONTEXT = 16
N_TENSOR = 16


def with_spikes(result, rng, source, target, parts, factor):
    owner, partner = [(jnp.arange(result.shape[axis_at]) // (result.shape[axis_at] // parts)).reshape([-1 if axis == axis_at else 1 for axis in range(result.ndim)]) for axis_at in (source, target)]
    chosen = jax.random.permutation(rng, parts)[partner]
    strong = (owner == chosen) | (owner == (partner + parts // 2) % parts)
    return jnp.where(strong, factor * result, result)


def block_levels(key, dims, cuts, low, top_value):
    loudness, own = 1.0, jax.random.fold_in(key, 6)
    for axis_at, parts in cuts:
        heights = jnp.exp(jax.random.uniform(jax.random.fold_in(own, axis_at), (parts,), jnp.float32, low / len(cuts), top_value / len(cuts)))
        loudness = loudness * jnp.repeat(heights, dims[axis_at] // parts).reshape([-1 if axis == axis_at else 1 for axis in range(len(dims))])
    return loudness


def gaussian(rng, extent, scale, limit, cuts=(), held_as=jnp.bfloat16):
    values = jax.random.normal(rng, extent, jnp.float32) * scale
    if len(cuts) > 0:
        values = block_levels(rng, extent, cuts, -0.22, 0.18) * values
    return jnp.clip(values, min=-limit, max=limit).astype(held_as)


def heavy_noise(rng, dims, spread, limit, shards, heavy, kind=jnp.bfloat16):
    values = spread * jax.random.normal(rng, dims, jnp.float32)
    if shards:
        values = values * block_levels(rng, dims, shards, -0.22, 0.18)
    return jnp.clip(with_spikes(values, jax.random.fold_in(rng, 3), *heavy), -limit, limit).astype(kind)


def setup_inputs(seed: int = 0) -> dict:
    splits = jax.random.split(jax.random.key(seed), 8)
    return {
        "query_rows": gaussian(splits[0], (SEQ, D), 1.0, 6.0, ((0, 16), (1, 16))),
        "key_rows": gaussian(splits[1], (SEQ, D), 1.0, 6.0, ((0, 16), (1, 16))),
        "value_rows": gaussian(splits[2], (SEQ, D), 1.0, 6.0, ((0, 16), (1, 16))),
        "residue": gaussian(splits[3], (MODES, D), 0.5, 3.0, ((1, 16),), jnp.float32),
        "decay_rate": jnp.clip(jnp.exp(math.log(0.04) - 6.015181 * jax.random.uniform(splits[4], (MODES, D), jnp.float32) ** block_levels(splits[4], (MODES, D), ((1, 16),), -0.2, 0.2)), 9.765625145519152e-05, 0.04),
        "out_weight": heavy_noise(splits[5], (D, D), D ** -0.5, 0.09375, ((0, 16),), (0, 1, 16, 2.0)),
        "cotangent": heavy_noise(splits[6], (SEQ, D), 1.0, 6.0, ((0, 16), (1, 16)), (0, 1, 16, 2.0)),
    }


def reference(query_rows, key_rows, value_rows, residue, decay_rate, out_weight, cotangent):
    width = D // N_TENSOR
    rows = SEQ // N_CONTEXT
    times = jnp.arange(SEQ).astype(jnp.float32)

    def add_mode(total, mode):
        weight_row, rate_row = mode
        term = (weight_row * jnp.sqrt(rate_row))[None, :] * jnp.exp(-rate_row[None, :] * times[:, None])
        return (total + term, None)
    kernel, _ = lax.scan(add_mode, jnp.zeros((SEQ, D), jnp.float32), (residue, decay_rate))
    length = 2 * SEQ
    kernel_hat = jnp.fft.rfft(kernel, n=length, axis=0)
    source = key_rows.astype(jnp.float32) * value_rows.astype(jnp.float32)
    conv = jnp.fft.irfft(jnp.fft.rfft(source, n=length, axis=0) * kernel_hat, n=length, axis=0)[:SEQ].astype(jnp.float32)
    gated = (query_rows.astype(jnp.float32) * conv).astype(jnp.bfloat16)
    gated_blocks = gated.reshape(SEQ, N_TENSOR, width).transpose(1, 0, 2)
    weight_blocks = out_weight.reshape(N_TENSOR, width, D)

    def add_channels(total, pair):
        block, weights = pair
        term = lax.optimization_barrier(jnp.dot(block, weights, preferred_element_type=jnp.float32).astype(jnp.bfloat16))
        return (total + term.astype(jnp.float32), None)
    mixed_sum, _ = lax.scan(add_channels, jnp.zeros((SEQ, D), jnp.float32), (gated_blocks, weight_blocks))
    mixed_out = mixed_sum.astype(jnp.bfloat16)
    back = lax.dot_general(cotangent, out_weight, (((1,), (1,)), ((), ())), preferred_element_type=jnp.float32)
    query_grad = (back * conv).astype(jnp.bfloat16)
    conv_grad = back * query_rows.astype(jnp.float32)
    mix_grad = jnp.fft.irfft(jnp.conj(kernel_hat) * jnp.fft.rfft(conv_grad, n=length, axis=0), n=length, axis=0)[:SEQ].astype(jnp.float32)
    key_grad = (mix_grad * value_rows.astype(jnp.float32)).astype(jnp.bfloat16)
    value_grad = (mix_grad * key_rows.astype(jnp.float32)).astype(jnp.bfloat16)
    gated_rows_blocks = gated.reshape(N_CONTEXT, rows, D)
    cotangent_blocks = cotangent.reshape(N_CONTEXT, rows, D)

    def add_positions(total, pair):
        block, grads = pair
        term = lax.optimization_barrier(lax.dot_general(block, grads, (((0,), (0,)), ((), ())), preferred_element_type=jnp.float32).astype(jnp.bfloat16))
        return (total + term.astype(jnp.float32), None)
    weight_sum, _ = lax.scan(add_positions, jnp.zeros((D, D), jnp.float32), (gated_rows_blocks, cotangent_blocks))
    weight_grad = weight_sum.astype(jnp.bfloat16)
    return (mixed_out, query_grad, key_grad, value_grad, weight_grad)
```

```python
import functools
import math

import jax
import jax.numpy as jnp
from jax import lax
from jax.experimental import pallas as pl
from jax.experimental.pallas import tpu as pltpu
from jax.sharding import PartitionSpec as P

MESH = pl.DeviceIdType.MESH
F32 = jnp.float32
BF16 = jnp.bfloat16
LANES = 128


def body(
    X, Y, Z,
    q_ref, k_ref, v_ref, res_ref, dec_ref, w_ref, cot_ref,
    mixed_ref, qg_ref, kg_ref, vg_ref, wg_ref,
    wv, cot_all, cot_t, gat, part, sib, rs_out, rs_in, st_f, st_g,
    src, cgr, conv, back, mix, kpad, krev, wacc, rates, weights, steps, starts,
    w_sem, ag_ss, ag_rs, cs_ss, cs_rs, aa_ss, aa_rs, fw_ss, fw_rs, st_ss, st_rs,
    g1_ss, g1_rs, g2_ss, g2_rs, sb_ss, sb_rs, rr_ss, rr_rs,
):
    N = X * Y
    R, C = q_ref.shape
    M = dec_ref.shape[0]
    T = R // 8
    G = C // LANES
    H = Z // 2
    c = lax.axis_index("context")
    j = lax.axis_index("tensor")
    z, r = j // 2, j % 2
    cx, cy = c // Y, c % Y
    other = z * 2 + 1 - r
    mine = (c, j)
    sibling = (c, other)
    zdev = [(c, ((z + 1) % Z) * 2 + r), (c, ((z + Z - 1) % Z) * 2 + r)]
    xdev = [(((cx + 1) % X) * Y + cy, j), (((cx + X - 1) % X) * Y + cy, j)]
    ydev = [(cx * Y + (cy + 1) % Y, j), (cx * Y + (cy + Y - 1) % Y, j)]

    def copy(source, target, send_sem, recv_sem, device):
        return pltpu.make_async_remote_copy(
            src_ref=source, dst_ref=target, send_sem=send_sem, recv_sem=recv_sem,
            device_id=device, device_id_type=MESH,
        )

    def lanes_of(g):
        return pl.ds(pl.multiple_of(g * LANES, LANES), LANES)

    def w_copy(n):
        return pltpu.make_async_copy(
            w_ref.at[:, pl.ds(pl.multiple_of(n * C, LANES), C)], wv.at[n], w_sem.at[n]
        )

    @pl.loop(0, 2 * Z)
    def _(n):
        w_copy(n).start()

    barrier = pltpu.get_barrier_semaphore()
    for device in zdev + [sibling]:
        pl.semaphore_signal(barrier, inc=1, device_id=device, device_id_type=MESH)

    @pl.loop(0, N)
    def _(p):
        @pl.when(p != c)
        def _():
            pl.semaphore_signal(barrier, inc=1, device_id=(p, j), device_id_type=MESH)

    rows8 = lax.broadcasted_iota(jnp.int32, (8, LANES), 0).astype(F32)

    def spread_modes():
        weight = res_ref[...] * jnp.sqrt(dec_ref[...])
        for m in range(M):
            rate = jnp.broadcast_to(dec_ref[pl.ds(m, 1), :], (8, C))
            rates[m] = rate
            steps[m] = jnp.exp(-8.0 * rate)
            weights[m] = jnp.broadcast_to(weight[m : m + 1], (8, C))

    def local_states(values, forward, out, place):
        @pl.loop(0, G)
        def _(g):
            lanes = lanes_of(g)
            tiles = [values[pl.ds(8 * a, 8), lanes] for a in range(T)]
            if not forward:
                tiles = tiles[::-1]

            @pl.loop(0, M // 8)
            def _(eight):
                sums = []
                for inner in range(8):
                    m = eight * 8 + inner
                    step = steps[m, :, lanes]
                    total = tiles[0]
                    for tile in tiles[1:]:
                        total = total * step + tile
                    reach = 7.0 - rows8 if forward else rows8
                    total = total * jnp.exp(-rates[m, :, lanes] * reach)
                    sums.append(jnp.sum(total, axis=0, keepdims=True))
                modes = pl.ds(pl.multiple_of(eight * 8, 8), 8)
                out[place, modes, lanes] = jnp.concatenate(sums, axis=0)

    def filter_tables():
        kpad[pl.ds(0, 8), :] = jnp.zeros((8, C), F32)
        krev[pl.ds(R, 8), :] = jnp.zeros((8, C), F32)

        @pl.loop(0, G)
        def _(g):
            lanes = lanes_of(g)

            def add_mode(m, tiles):
                rate, weight, step = rates[m, :, lanes], weights[m, :, lanes], steps[m, :, lanes]
                ahead = weight * jnp.exp(-rate * rows8)
                behind = weight * jnp.exp(-rate * (7.0 - rows8))
                new = []
                for a in range(T):
                    new.append((tiles[a][0] + ahead, tiles[a][1] + behind))
                    ahead = ahead * step
                    behind = behind * step
                return tuple(new)

            zero = jnp.zeros((8, LANES), F32)
            tiles = lax.fori_loop(0, M, add_mode, tuple((zero, zero) for _ in range(T)))
            for a in range(T):
                kpad[pl.ds(8 + 8 * a, 8), lanes] = tiles[a][0]
                krev[pl.ds(8 * (T - 1 - a), 8), lanes] = tiles[a][1]

    def toeplitz(values, forward, out):
        @pl.loop(0, G)
        def _(g):
            lanes = lanes_of(g)
            total = [jnp.zeros((8, LANES), F32) for _ in range(T)]
            for b in range(8):
                if forward:
                    taps = [kpad[pl.ds(8 + 8 * n - b, 8), lanes] for n in range(T)]
                else:
                    taps = [krev[pl.ds(R - 1 - 8 * n - b, 8), lanes] for n in range(T)]
                for u in range(T):
                    row = jnp.broadcast_to(values[pl.ds(8 * u + b, 1), lanes], (8, LANES))
                    for a in range(u, T) if forward else range(u + 1):
                        total[a] = total[a] + taps[abs(a - u)] * row
            for a in range(T):
                out[pl.ds(8 * a, 8), lanes] = total[a]

    def carry_in(states, forward):
        decay = jnp.exp(-float(R) * dec_ref[...])

        def step(n, total):
            p = n if forward else N - 1 - n
            return total * decay + states[p]

        count = c if forward else N - 1 - c
        total = lax.fori_loop(0, count, step, jnp.zeros((M, C), F32))
        for m in range(M):
            starts[m] = weights[m] * total[m : m + 1]

    def add_carry(forward, out):
        @pl.loop(0, G)
        def _(g):
            lanes = lanes_of(g)

            def add_mode(m, tiles):
                rate, step = rates[m, :, lanes], steps[m, :, lanes]
                term = starts[m, :, lanes] * jnp.exp(-rate * ((rows8 + 1.0) if forward else (8.0 - rows8)))
                new = []
                for a in range(T):
                    new.append(tiles[a] + term)
                    term = term * step
                return tuple(new)

            order = list(range(T)) if forward else list(range(T))[::-1]
            tiles = lax.fori_loop(
                0, M, add_mode, tuple(out[pl.ds(8 * a, 8), lanes] for a in order)
            )
            for n, a in enumerate(order):
                out[pl.ds(8 * a, 8), lanes] = tiles[n]

    def state_copy(states, way, p, owner):
        return copy(
            states.at[owner], states.at[owner], st_ss.at[way, p], st_rs.at[way, owner], (p, j)
        )

    def send_states(states, way):
        lo, hi = (c + 1, N) if way == 0 else (0, c)

        @pl.loop(lo, hi)
        def _(p):
            state_copy(states, way, p, c).start()

    def wait_states(states, way):
        lo, hi = (0, c) if way == 0 else (c + 1, N)

        @pl.loop(lo, hi)
        def _(p):
            state_copy(states, way, c, p).wait_recv()

    def drain_states(states, way):
        lo, hi = (c + 1, N) if way == 0 else (0, c)

        @pl.loop(lo, hi)
        def _(p):
            state_copy(states, way, p, c).wait_send()

    def piece(way, hop, last, size):
        if hop < last:
            return pl.ds(0, size)
        return pl.ds(way * (size // 2), size // 2)

    def ag_copy(way, hop, sending):
        away = hop - 1 if sending else hop
        owner = (z - away + Z) % Z if way == 0 else (z + away) % Z
        rows = piece(way, hop, H, R)
        ref = cot_all.at[owner * 2 + r, rows]
        return copy(ref, ref, ag_ss.at[way, hop - 1], ag_rs.at[way, hop - 1], zdev[way])

    def cs_copy(zz, sending):
        ref = cot_all.at[zz * 2 + (r if sending else 1 - r)]
        return copy(ref, ref, cs_ss.at[zz], cs_rs.at[zz], sibling)

    def aa_copy(zz):
        owner = zz * 2 + r
        return copy(
            cot_all.at[owner], cot_t.at[cx, cy], aa_ss.at[zz], aa_rs.at[c], (owner, j)
        )

    def spread(zz):
        cs_copy(zz, True).start()

        @pl.when(zz * 2 + r != c)
        def _():
            aa_copy(zz).start()

    def ag_send(hop):
        for way in range(2):
            ag_copy(way, hop, True).start()

    def ag_arrive(hop):
        for way in range(2):
            ag_copy(way, hop, False).wait_recv()
        if hop < H:
            ag_send(hop + 1)
            spread((z - hop + Z) % Z)
        spread((z + hop) % Z)

    half = R // 2

    def g1_copy(part_at, way, hop, sending):
        size, last, devices, at = (X, X // 2, xdev, cx) if part_at == 0 else (Y, Y // 2, ydev, cy)
        away = hop - 1 if sending else hop
        owner = (at - away + size) % size if way == 0 else (at + away) % size
        low = part_at * half
        if hop == last:
            rows = pl.ds(low + way * (half // 2), half // 2)
        else:
            rows = pl.ds(low, half)
        ref = gat.at[owner, cy, rows] if part_at == 0 else gat.at[cx, owner, rows]
        return copy(ref, ref, g1_ss.at[part_at, way, hop - 1], g1_rs.at[part_at, way, hop - 1], devices[way])

    def g2_copy(part_at, way, hop, sending):
        size, last, devices, at, many = (
            (Y, Y // 2, ydev, cy, X) if part_at == 0 else (X, X // 2, xdev, cx, Y)
        )
        away = hop - 1 if sending else hop
        owner = (at - away + size) % size if way == 0 else (at + away) % size
        group = piece(way, hop, last, many)
        rows = pl.ds(part_at * half, half)
        ref = gat.at[group, owner, rows] if part_at == 0 else gat.at[owner, group, rows]
        return copy(ref, ref, g2_ss.at[part_at, way, hop - 1], g2_rs.at[part_at, way, hop - 1], devices[way])

    def hops_of(phase, part_at):
        return (X // 2, Y // 2)[part_at if phase == 1 else 1 - part_at]

    def gather_send(phase, hop):
        make = g1_copy if phase == 1 else g2_copy
        for part_at in range(2):
            if hop <= hops_of(phase, part_at):
                for way in range(2):
                    make(part_at, way, hop, True).start()

    def gather_wait(phase, hop):
        make = g1_copy if phase == 1 else g2_copy
        for part_at in range(2):
            if hop <= hops_of(phase, part_at):
                for way in range(2):
                    make(part_at, way, hop, False).wait_recv()

    def sb_copy(zz, sending):
        target = zz * 2 + (1 - r if sending else r)
        return copy(part.at[target], sib.at[zz], sb_ss.at[zz], sb_rs.at[zz], sibling)

    def project(lo, hi):
        @pl.loop(lo, hi)
        def _(o):
            hop = H - (o + 1) // 2
            zz = (z + Z + hop * (2 * (o % 2) - 1)) % Z
            gated = gat[cx, cy]
            for core in range(2):
                target = zz * 2 + ((1 - r) if core == 0 else r)
                part[target] = jnp.dot(
                    gated, wv[target], preferred_element_type=F32
                ).astype(BF16)
                if core == 0:
                    sb_copy(zz, True).start()

    def rr_copy(way, step):
        rows = pl.ds(way * half, half) if step == 0 else pl.ds(0, R)
        return copy(
            rs_out.at[way, step, rows], rs_in.at[way, step, rows],
            rr_ss.at[way, step], rr_rs.at[way, step], zdev[way],
        )

    def pair_sum(zz):
        return part[zz * 2 + r].astype(F32) + sib[zz].astype(F32)

    def reduce_step(step):
        if step == 0:
            zz = (z + H) % Z
            sb_copy(zz, False).wait_recv()
            total = pair_sum(zz).astype(BF16)
            for way in range(2):
                rows = slice(way * half, (way + 1) * half)
                rs_out[way, 0, rows] = total[rows]
                rr_copy(way, 0).start()
            return
        for way in range(2):
            away = H - step
            zz = (z + away) % Z if way == 0 else (z - away + Z) % Z
            sb_copy(zz, False).wait_recv()
            rr_copy(way, step - 1).wait_recv()
            add_arrived(way, step, pair_sum(zz), rs_out.at[way, step])
            rr_copy(way, step).start()

    def add_arrived(way, step, total, out):
        if step == 1:
            for part_at in range(2):
                rows = slice(part_at * half, (part_at + 1) * half)
                value = total[rows]
                if part_at == way:
                    value = value + rs_in[way, 0, rows].astype(F32)
                out[rows] = value.astype(BF16)
        else:
            out[...] = (total + rs_in[way, step - 1].astype(F32)).astype(BF16)

    def reduce_last():
        sb_copy(z, False).wait_recv()
        for way in range(2):
            rr_copy(way, H - 1).wait_recv()
        total = pair_sum(z)
        if H == 1:
            for way in range(2):
                rows = slice(way * half, (way + 1) * half)
                mixed_ref[rows] = (total[rows] + rs_in[way, 0, rows].astype(F32)).astype(BF16)
        else:
            total = total + rs_in[0, H - 1].astype(F32) + rs_in[1, H - 1].astype(F32)
            mixed_ref[...] = total.astype(BF16)

    spread_modes()
    src[...] = k_ref[...].astype(F32) * v_ref[...].astype(F32)
    cot_all[j] = cot_ref[...]
    local_states(src, True, st_f, c)
    pl.semaphore_wait(barrier, N - 1 + 3)
    ag_send(1)
    send_states(st_f, 0)
    spread(z)
    filter_tables()
    toeplitz(src, True, conv)
    if H > 1:
        ag_arrive(1)
    wait_states(st_f, 0)
    carry_in(st_f, True)
    add_carry(True, conv)
    gat[cx, cy] = (q_ref[...].astype(F32) * conv[...]).astype(BF16)
    gather_send(1, 1)
    if H > 2:
        ag_arrive(2)

    @pl.loop(0, 2 * Z)
    def _(n):
        w_copy(n).wait()

    project(0, min(3, Z))
    reduce_step(0)
    gather_wait(1, 1)
    top = max(X // 2, Y // 2)
    for hop in range(2, top + 1):
        gather_send(1, hop)
    if H > 3:
        ag_arrive(3)
    project(min(3, Z), Z)
    for hop in range(2, top + 1):
        gather_wait(1, hop)
    gather_send(2, 1)
    if H > 1:
        reduce_step(1)
    ag_arrive(H)
    @pl.loop(0, Z)
    def _(zz):
        cs_copy(zz, False).wait_recv()

    back[...] = jnp.zeros((R, C), F32)

    @pl.loop(0, 2 * Z)
    def _(n):
        back[...] += lax.dot_general(
            cot_all[n], wv[n], (((1,), (1,)), ((), ())), preferred_element_type=F32
        )

    if H > 2:
        reduce_step(2)
    qg_ref[...] = (back[...] * conv[...]).astype(BF16)
    cgr[...] = back[...] * q_ref[...].astype(F32)
    local_states(cgr, False, st_g, c)
    send_states(st_g, 1)
    gather_wait(2, 1)
    for hop in range(2, top + 1):
        gather_send(2, hop)
    toeplitz(cgr, False, mix)
    if H > 3:
        reduce_step(3)
    for step in range(4, H):
        reduce_step(step)
    active = c % 2 == r

    def fw_copy(p):
        ref = cot_t.at[p // Y, p % Y]
        return copy(ref, ref, fw_ss.at[p], fw_rs.at[p], sibling)

    def each_other(act):
        @pl.loop(0, N)
        def _(p):
            @pl.when(p != c)
            def _():
                act(p)

    def forward_one(p):
        copy(
            cot_all.at[p], cot_t.at[p // Y, p % Y], aa_ss.at[0], aa_rs.at[p], mine
        ).wait_recv()
        fw_copy(p).start()

    @pl.when(active)
    def _():
        each_other(forward_one)

    wait_states(st_g, 1)
    carry_in(st_g, False)
    add_carry(False, mix)
    kg_ref[...] = (mix[...] * v_ref[...].astype(F32)).astype(BF16)
    vg_ref[...] = (mix[...] * k_ref[...].astype(F32)).astype(BF16)
    reduce_last()

    @pl.when(jnp.logical_not(active))
    def _():
        each_other(lambda p: fw_copy(p).wait_recv())

    cot_t[cx, cy] = cot_all[c]
    for hop in range(2, top + 1):
        gather_wait(2, hop)
    wacc[...] = jnp.zeros((C, C), F32)

    @pl.loop(0, X)
    def _(n):
        wacc[...] += lax.dot_general(
            gat[n].reshape(Y * R, C), cot_t[n].reshape(Y * R, C),
            (((0,), (0,)), ((), ())), preferred_element_type=F32,
        )

    wg_ref[...] = wacc[...].astype(BF16)

    drain_states(st_f, 0)
    drain_states(st_g, 1)
    for way in range(2):
        for hop in range(1, H + 1):
            ag_copy(way, hop, True).wait_send()
            rr_copy(way, hop - 1).wait_send()
        for phase, make in ((1, g1_copy), (2, g2_copy)):
            for part_at in range(2):
                for hop in range(1, hops_of(phase, part_at) + 1):
                    make(part_at, way, hop, True).wait_send()

    @pl.loop(0, Z)
    def _(zz):
        cs_copy(zz, True).wait_send()
        sb_copy(zz, True).wait_send()

        @pl.when(zz * 2 + r != c)
        def _():
            aa_copy(zz).wait_send()

    @pl.when(active)
    def _():
        each_other(lambda p: fw_copy(p).wait_send())


def solution(mesh):
    N = mesh.shape["context"]
    X = math.isqrt(N)
    Y = N // X
    Z = mesh.shape["tensor"] // 2
    H = Z // 2

    def shards(query_rows, key_rows, value_rows, residue, decay_rate, out_weight, cotangent):
        R, C = query_rows.shape
        M = residue.shape[0]
        small = jax.ShapeDtypeStruct((R, C), BF16)
        vmem = pl.BlockSpec(memory_space=pltpu.VMEM)
        dma = pltpu.SemaphoreType.DMA
        top = max(X // 2, Y // 2)
        return pl.pallas_call(
            functools.partial(body, X, Y, Z),
            out_shape=(small, small, small, small, jax.ShapeDtypeStruct((C, C), BF16)),
            in_specs=[vmem] * 5 + [pl.BlockSpec(memory_space=pl.ANY), vmem],
            out_specs=(vmem,) * 5,
            scratch_shapes=[
                pltpu.VMEM((2 * Z, C, C), BF16),
                pltpu.VMEM((2 * Z, R, C), BF16),
                pltpu.VMEM((X, Y, R, C), BF16),
                pltpu.VMEM((X, Y, R, C), BF16),
                pltpu.VMEM((2 * Z, R, C), BF16),
                pltpu.VMEM((Z, R, C), BF16),
                pltpu.VMEM((2, H, R, C), BF16),
                pltpu.VMEM((2, H, R, C), BF16),
                pltpu.VMEM((N, M, C), F32),
                pltpu.VMEM((N, M, C), F32),
                pltpu.VMEM((R, C), F32),
                pltpu.VMEM((R, C), F32),
                pltpu.VMEM((R, C), F32),
                pltpu.VMEM((R, C), F32),
                pltpu.VMEM((R, C), F32),
                pltpu.VMEM((R + 8, C), F32),
                pltpu.VMEM((R + 8, C), F32),
                pltpu.VMEM((C, C), F32),
                pltpu.VMEM((M, 8, C), F32),
                pltpu.VMEM((M, 8, C), F32),
                pltpu.VMEM((M, 8, C), F32),
                pltpu.VMEM((M, 8, C), F32),
                dma((2 * Z,)),
                dma((2, H)),
                dma((2, H)),
                dma((Z,)),
                dma((Z,)),
                dma((Z,)),
                dma((N,)),
                dma((N,)),
                dma((N,)),
                dma((2, N)),
                dma((2, N)),
                dma((2, 2, top)),
                dma((2, 2, top)),
                dma((2, 2, top)),
                dma((2, 2, top)),
                dma((Z,)),
                dma((Z,)),
                dma((2, H)),
                dma((2, H)),
            ],
            compiler_params=pltpu.CompilerParams(
                collective_id=0, has_side_effects=True, vmem_limit_bytes=56 * 1024 * 1024
            ),
            name="hyena_block",
        )(query_rows, key_rows, value_rows, residue, decay_rate, out_weight, cotangent)

    placed = (
        P("context", "tensor"),
        P("context", "tensor"),
        P("context", "tensor"),
        P(None, "tensor"),
        P(None, "tensor"),
        P("tensor", None),
        P("context", "tensor"),
    )
    return jax.shard_map(
        shards,
        mesh=mesh,
        in_specs=placed,
        out_specs=(
            P("context", "tensor"),
            P("context", "tensor"),
            P("context", "tensor"),
            P("context", "tensor"),
            P("tensor", "context"),
        ),
        check_vma=False,
    )
```

```python
import functools
import math

import jax
import jax.numpy as jnp
import ml_dtypes
import numpy as np
from jax import lax
from jax.experimental import pallas as pl
from jax.experimental.pallas import tpu as pltpu
from jax.sharding import PartitionSpec as P

MESH = pl.DeviceIdType.MESH
F32 = jnp.float32
BF16 = jnp.bfloat16
LANES = 128


def body(
    X, Y, Z,
    q_in, k_in, v_in, res_in, dec_in, w_ref, cot_in, fold_in, unfold_in,
    mixed_ref, qg_ref, kg_ref, vg_ref, wg_ref,
    wv, cot_all, cot_t, gat, part, sib, rs_out, rs_in, states, row_states,
    q_ref, k_ref, v_ref, res_ref, dec_ref, fold, unfold, in_sem,
    src, cgr, conv, back, mix, taps, taps_hat, wacc, rates, weights, powers, starts,
    mixed_buf, qg_buf, kg_buf, vg_buf, wg_buf, out_sem,
    w_sem, ag_ss, ag_rs, cs_ss, cs_rs, aa_ss, aa_rs, fw_ss, fw_rs, ex_ss, ex_rs, st_ss, st_rs, ro_ss, ro_rs,
    g1_ss, g1_rs, g2_ss, g2_rs, sb_ss, sb_rs, rr_ss, rr_rs,
):
    N = X * Y
    R, C = q_in.shape
    M = dec_in.shape[0]
    T = R // 8
    G = C // LANES
    H = Z // 2
    c = lax.axis_index("context")
    j = lax.axis_index("tensor")
    z, r = j // 2, j % 2
    cx, cy = c // Y, c % Y
    other = z * 2 + 1 - r
    mine = (c, j)
    sibling = (c, other)
    zdev = [(c, ((z + 1) % Z) * 2 + r), (c, ((z + Z - 1) % Z) * 2 + r)]
    xdev = [(((cx + 1) % X) * Y + cy, j), (((cx + X - 1) % X) * Y + cy, j)]
    ydev = [(cx * Y + (cy + 1) % Y, j), (cx * Y + (cy + Y - 1) % Y, j)]

    def copy(source, target, send_sem, recv_sem, device):
        return pltpu.make_async_remote_copy(
            src_ref=source, dst_ref=target, send_sem=send_sem, recv_sem=recv_sem,
            device_id=device, device_id_type=MESH,
        )

    def lanes_of(g):
        return pl.ds(pl.multiple_of(g * LANES, LANES), LANES)

    barrier = pltpu.get_barrier_semaphore()
    for device in zdev + [sibling]:
        pl.semaphore_signal(barrier, inc=1, device_id=device, device_id_type=MESH)

    @pl.loop(0, N)
    def _(p):
        @pl.when(p != c)
        def _():
            pl.semaphore_signal(barrier, inc=1, device_id=(p, j), device_id_type=MESH)

    loads = (
        (k_in, k_ref), (v_in, v_ref), (dec_in, dec_ref), (cot_in, cot_all.at[j]), (res_in, res_ref),
        (fold_in, fold), (q_in, q_ref), (unfold_in, unfold),
    )

    def load(n):
        return pltpu.make_async_copy(*loads[n], in_sem.at[n])

    for n in range(len(loads)):
        load(n).start()

    def w_copy(n):
        return pltpu.make_async_copy(
            w_ref.at[:, pl.ds(pl.multiple_of(n * C, LANES), C)], wv.at[n], w_sem.at[n]
        )

    @pl.loop(0, 2 * Z)
    def _(n):
        w_copy(n).start()

    rows8 = lax.broadcasted_iota(jnp.int32, (8, LANES), 0).astype(F32)

    def spread_weights():
        load(4).wait()
        weight = res_ref[...] * jnp.sqrt(dec_ref[...])
        for m in range(M):
            weights[m] = jnp.broadcast_to(weight[m : m + 1], (8, C))

    def spread_rates():
        for m in range(M):
            rate = jnp.broadcast_to(dec_ref[pl.ds(m, 1), :], (8, C))
            rates[m] = rate
            powers[m] = jnp.exp(-8.0 * rate)

    def local_states(values, forward):
        way = 0 if forward else 1

        @pl.loop(0, G)
        def _(g):
            lanes = lanes_of(g)
            tiles = [values[pl.ds(8 * a, 8), lanes] for a in range(T)]
            if not forward:
                tiles = tiles[::-1]

            @pl.loop(0, M // 8)
            def _(eight):
                sums = []
                for inner in range(8):
                    m = eight * 8 + inner
                    step = powers[m, :, lanes]
                    total = tiles[0]
                    for tile in tiles[1:]:
                        total = total * step + tile
                    reach = 7.0 - rows8 if forward else rows8
                    total = total * jnp.exp(-rates[m, :, lanes] * reach)
                    sums.append(jnp.sum(total, axis=0, keepdims=True))
                modes = pl.ds(pl.multiple_of(eight * 8, 8), 8)
                states[way, cy, modes, lanes] = jnp.concatenate(sums, axis=0)

    def filter_taps():
        @pl.loop(0, G)
        def _(g):
            lanes = lanes_of(g)

            def add_mode(m, tiles):
                step = powers[m, :, lanes]
                term = weights[m, :, lanes] * jnp.exp(-rates[m, :, lanes] * rows8)
                new = []
                for a in range(T):
                    new.append(tiles[a] + term)
                    term = term * step
                return tuple(new)

            zero = jnp.zeros((8, LANES), F32)
            tiles = lax.fori_loop(0, M, add_mode, (zero,) * T, unroll=4)
            for a in range(T):
                taps[pl.ds(8 * a, 8), lanes] = tiles[a]

    width = min(C, 256)

    def halves(value):
        high = value.astype(BF16)
        return high, (value - high.astype(F32)).astype(BF16)

    def analyse(value):
        high, low = halves(value)
        return jnp.dot(fold[...], jnp.concatenate([high, high, low]), preferred_element_type=F32)

    def filter_spectrum():
        for lo in range(0, C, width):
            lanes = slice(lo, lo + width)
            taps_hat[:, lanes] = analyse(taps[:, lanes])

    def convolve(values, forward, out):
        for lo in range(0, C, width):
            lanes = slice(lo, lo + width)
            both = analyse(values[:, lanes])
            real, imag = both[:R], both[R:]
            tap_real, tap_imag = taps_hat[:R, lanes], taps_hat[R:, lanes]
            if forward:
                new_real = tap_real * real - tap_imag * imag
                new_imag = tap_real * imag + tap_imag * real
            else:
                new_real = tap_real * real + tap_imag * imag
                new_imag = tap_real * imag - tap_imag * real
            real_high, real_low = halves(new_real)
            imag_high, imag_low = halves(new_imag)
            out[:, lanes] = jnp.dot(
                unfold[...],
                jnp.concatenate([real_high, imag_high, real_high, imag_high, real_low, imag_low]),
                preferred_element_type=F32,
            )

    def carry_in(forward):
        way = 0 if forward else 1
        decay = jnp.exp(-float(R) * dec_ref[...])
        row_decay = jnp.exp(-float(R * Y) * dec_ref[...])

        def add_row(n, total):
            return total * row_decay + row_states[way, n if forward else X - 1 - n]

        def add_block(n, total):
            return total * decay + states[way, n if forward else Y - 1 - n]

        total = lax.fori_loop(0, cx if forward else X - 1 - cx, add_row, jnp.zeros((M, C), F32))
        total = lax.fori_loop(0, cy if forward else Y - 1 - cy, add_block, total)
        for m in range(M):
            starts[m] = weights[m] * total[m : m + 1]

    def add_carry(forward, out):
        @pl.loop(0, G)
        def _(g):
            lanes = lanes_of(g)

            def add_mode(m, tiles):
                rate, step = rates[m, :, lanes], powers[m, :, lanes]
                term = starts[m, :, lanes] * jnp.exp(-rate * ((rows8 + 1.0) if forward else (8.0 - rows8)))
                new = []
                for a in range(T):
                    new.append(tiles[a] + term)
                    term = term * step
                return tuple(new)

            order = list(range(T)) if forward else list(range(T))[::-1]
            tiles = lax.fori_loop(
                0, M, add_mode, tuple(out[pl.ds(8 * a, 8), lanes] for a in order), unroll=4
            )
            for n, a in enumerate(order):
                out[pl.ds(8 * a, 8), lanes] = tiles[n]

    def state_copy(way, y, sending):
        ref = states.at[way, cy if sending else y]
        sem = st_rs.at[way, cy if sending else y]
        return copy(ref, ref, st_ss.at[way, y], sem, (cx * Y + y, j))

    def row_copy(way, x, sending):
        ref = row_states.at[way, cx if sending else x]
        sem = ro_rs.at[way, cx if sending else x]
        return copy(ref, ref, ro_ss.at[way, x], sem, (x * Y + cy, j))

    def others(count, here, act):
        @pl.loop(0, count)
        def _(n):
            pl.when(n != here)(lambda: act(n))

    def later(way):
        return (cx + 1, X) if way == 0 else (0, cx)

    def sooner(way):
        return (0, cx) if way == 0 else (cx + 1, X)

    def send_states(way):
        others(Y, cy, lambda y: state_copy(way, y, True).start())

    def send_rows(way):
        others(Y, cy, lambda y: state_copy(way, y, False).wait_recv())
        decay = jnp.exp(-float(R) * dec_ref[...])
        order = range(Y) if way == 0 else range(Y)[::-1]
        total = states[way, order[0]]
        for y in order[1:]:
            total = total * decay + states[way, y]
        row_states[way, cx] = total

        @pl.loop(*later(way))
        def _(x):
            row_copy(way, x, True).start()

    def wait_rows(way):
        @pl.loop(*sooner(way))
        def _(x):
            row_copy(way, x, False).wait_recv()

    def drain_states(way):
        others(Y, cy, lambda y: state_copy(way, y, True).wait_send())

        @pl.loop(*later(way))
        def _(x):
            row_copy(way, x, True).wait_send()

    def piece(way, hop, last, size):
        if hop < last:
            return pl.ds(0, size)
        return pl.ds(way * (size // 2), size // 2)

    def ag_copy(way, hop, k, sending):
        away = hop - 1 if sending else hop
        owner = (z - away + Z) % Z if way == 0 else (z + away) % Z
        ref = cot_all.at[owner * 2 + r, pl.ds(k * (R // 2), R // 2)]
        return copy(ref, ref, ag_ss.at[way, hop - 1, k], ag_rs.at[way, hop - 1, k], zdev[way])

    def ag_pieces(hop):
        return [(way, k) for k in range(2) for way in range(2) if hop < H or way == k]

    def cs_copy(zz, sending):
        ref = cot_all.at[zz * 2 + (r if sending else 1 - r)]
        return copy(ref, ref, cs_ss.at[zz], cs_rs.at[zz], sibling)

    odd = z % 2
    own_rows = pl.ds(pl.multiple_of(odd * (R // 2), R // 2), R // 2)
    other_rows = pl.ds(pl.multiple_of((1 - odd) * (R // 2), R // 2), R // 2)

    def aa_copy(zz):
        owner = zz * 2 + r
        return copy(
            cot_all.at[owner, own_rows], cot_t.at[cx, cy, own_rows], aa_ss.at[zz], aa_rs.at[c], (owner, j)
        )

    def spread(zz):
        cs_copy(zz, True).start()

    def scatter(lo, hi):
        count = hi - lo

        @pl.loop(0, count)
        def _(n):
            zz = (z + Z + lo + (c // 2 + n) % count) % Z

            @pl.when(zz * 2 + r != c)
            def _():
                aa_copy(zz).start()

    def ag_start():
        for way, k in ag_pieces(1):
            ag_copy(way, 1, k, True).start()

    def ag_arrive(hop, half_at):
        for way, k in ag_pieces(hop):
            if k == half_at:
                ag_copy(way, hop, k, False).wait_recv()
                if (way, k) in ag_pieces(hop + 1) and hop < H:
                    ag_copy(way, hop + 1, k, True).start()
        if half_at == 1:
            spread((z + hop) % Z)
            if hop < H:
                spread((z - hop + Z) % Z)

    half = R // 2

    def g1_copy(part_at, way, hop, sending):
        size, last, devices, at = (X, X // 2, xdev, cx) if part_at == 0 else (Y, Y // 2, ydev, cy)
        away = hop - 1 if sending else hop
        owner = (at - away + size) % size if way == 0 else (at + away) % size
        low = part_at * half
        if hop == last:
            rows = pl.ds(low + way * (half // 2), half // 2)
        else:
            rows = pl.ds(low, half)
        ref = gat.at[owner, cy, rows] if part_at == 0 else gat.at[cx, owner, rows]
        return copy(ref, ref, g1_ss.at[part_at, way, hop - 1], g1_rs.at[part_at, way, hop - 1], devices[way])

    def g2_copy(part_at, way, hop, sending):
        size, last, devices, at, many = (
            (Y, Y // 2, ydev, cy, X) if part_at == 0 else (X, X // 2, xdev, cx, Y)
        )
        away = hop - 1 if sending else hop
        owner = (at - away + size) % size if way == 0 else (at + away) % size
        group = piece(way, hop, last, many)
        rows = pl.ds(part_at * half, half)
        ref = gat.at[group, owner, rows] if part_at == 0 else gat.at[owner, group, rows]
        return copy(ref, ref, g2_ss.at[part_at, way, hop - 1], g2_rs.at[part_at, way, hop - 1], devices[way])

    def hops_of(phase, part_at):
        return (X // 2, Y // 2)[part_at if phase == 1 else 1 - part_at]

    def gather_send(phase, hop):
        make = g1_copy if phase == 1 else g2_copy
        for part_at in range(2):
            if hop <= hops_of(phase, part_at):
                for way in range(2):
                    make(part_at, way, hop, True).start()

    def gather_wait(phase, hop):
        make = g1_copy if phase == 1 else g2_copy
        for part_at in range(2):
            if hop <= hops_of(phase, part_at):
                for way in range(2):
                    make(part_at, way, hop, False).wait_recv()

    def sb_copy(zz, sending):
        target = zz * 2 + (1 - r if sending else r)
        return copy(part.at[target], sib.at[zz], sb_ss.at[zz], sb_rs.at[zz], sibling)

    def project(lo, hi):
        @pl.loop(lo, hi)
        def _(o):
            hop = H - (o + 1) // 2
            zz = (z + Z + hop * (2 * (o % 2) - 1)) % Z
            gated = gat[cx, cy]
            for core in range(2):
                target = zz * 2 + ((1 - r) if core == 0 else r)
                part[target] = jnp.dot(
                    gated, wv[target], preferred_element_type=F32
                ).astype(BF16)
                if core == 0:
                    sb_copy(zz, True).start()

    halves_of = (pl.ds(0, half), pl.ds(half, half))

    def rr_copy(way, step, k):
        return copy(
            rs_out.at[way, step, halves_of[k]], rs_in.at[way, step, halves_of[k]],
            rr_ss.at[way, step, k], rr_rs.at[way, step, k], zdev[way],
        )

    def pair_sum(zz, k):
        return part[zz * 2 + r, halves_of[k]].astype(F32) + sib[zz, halves_of[k]].astype(F32)

    def reduce_target(way, step):
        away = H - step
        return (z + away) % Z if way == 0 else (z - away + Z) % Z

    def reduce_piece(way, step, k, arrived):
        total = pair_sum(reduce_target(way, step), k)
        if arrived:
            rr_copy(way, step - 1, k).wait_recv()
            total = total + rs_in[way, step - 1, halves_of[k]].astype(F32)
        rs_out[way, step, halves_of[k]] = total.astype(BF16)
        rr_copy(way, step, k).start()

    def reduce_first():
        sb_copy((z + H) % Z, False).wait_recv()
        for way in range(2):
            reduce_piece(way, 0, way, False)
        if H > 1:
            for way in range(2):
                sb_copy(reduce_target(way, 1), False).wait_recv()
                reduce_piece(way, 1, 1 - way, False)

    def reduce_second():
        if H > 1:
            for way in range(2):
                reduce_piece(way, 1, way, True)

    def reduce_step(step, k):
        if step < H:
            for way in range(2):
                if k == 0:
                    sb_copy(reduce_target(way, step), False).wait_recv()
                reduce_piece(way, step, k, True)

    def reduce_pieces():
        return [
            (way, step, k) for step in range(H) for way in range(2) for k in range(2)
            if step > 0 or k == way
        ]

    def reduce_last():
        sb_copy(z, False).wait_recv()
        for k in range(2):
            total = pair_sum(z, k)
            for way in range(2):
                if H > 1 or way == k:
                    rr_copy(way, H - 1, k).wait_recv()
                    total = total + rs_in[way, H - 1, halves_of[k]].astype(F32)
            mixed_buf[halves_of[k]] = total.astype(BF16)

    active = c % 2 == r

    def fw_copy(own, p):
        ref = cot_t.at[p // Y, p % Y, own_rows if own else other_rows]
        n = 0 if own else 1
        return copy(ref, ref, fw_ss.at[n, p], fw_rs.at[n, p], sibling)

    def ex_copy(way, p, sending):
        side = odd if sending else 1 - odd
        low = pl.multiple_of(side * (R // 2) + way * (R // 4), R // 4)
        ref = cot_t.at[p // Y, p % Y, pl.ds(low, R // 4)]
        return copy(ref, ref, ex_ss.at[way, p], ex_rs.at[way, p], zdev[way])

    def aa_arrived(p):
        ref = cot_t.at[p // Y, p % Y, own_rows]
        return copy(ref, ref, aa_ss.at[0], aa_rs.at[p], mine)

    def pass_one(p):
        aa_arrived(p).wait_recv()
        for way in range(2):
            ex_copy(way, p, True).start()
        fw_copy(True, p).start()

    def pass_on():
        pl.when(active)(lambda: others(N, c, pass_one))

    def hand_one(p):
        for way in range(2):
            ex_copy(way, p, False).wait_recv()
        fw_copy(False, p).start()

    def hand_over():
        pl.when(active)(lambda: others(N, c, hand_one))

    def handed_own():
        pl.when(jnp.logical_not(active))(
            lambda: others(N, c, lambda p: fw_copy(True, p).wait_recv())
        )
        cot_t[cx, cy] = cot_all[c]

    def handed_over():
        pl.when(jnp.logical_not(active))(
            lambda: others(N, c, lambda p: fw_copy(False, p).wait_recv())
        )

    def drain_one(p):
        for way in range(2):
            ex_copy(way, p, True).wait_send()
        fw_copy(True, p).wait_send()
        fw_copy(False, p).wait_send()

    def wait_weights():
        @pl.loop(0, 2 * Z)
        def _(n):
            w_copy(n).wait()

    def begin():
        for n in (0, 1, 2):
            load(n).wait()
        src[...] = k_ref[...].astype(F32) * v_ref[...].astype(F32)
        spread_rates()
        local_states(src, True)

    def first_sends():
        load(3).wait()
        ag_start()
        send_states(0)
        spread(z)

    def filter_spectrum_loaded():
        for n in (5, 6, 7):
            load(n).wait()
        filter_spectrum()

    def gate():
        carry_in(True)
        add_carry(True, conv)
        gat[cx, cy] = (q_ref[...].astype(F32) * conv[...]).astype(BF16)
        gather_send(1, 1)

    def multiply_back(distances, first=False):
        if not distances:
            return
        zs = [(z + Z + away) % Z for away in distances]
        blocks = [zz * 2 + core for zz in zs for core in range(2)]
        total = lax.dot_general(
            jnp.concatenate([cot_all[n] for n in blocks], axis=1),
            jnp.concatenate([wv[n] for n in blocks], axis=1),
            (((1,), (1,)), ((), ())), preferred_element_type=F32,
        )
        back[...] = total if first else back[...] + total

    def sibling_here(distances):
        for away in distances:
            cs_copy((z + Z + away) % Z, False).wait_recv()

    def back_states():
        qg_buf[...] = (back[...] * conv[...]).astype(BF16)
        put(0, qg_buf, qg_ref).start()
        cgr[...] = back[...] * q_ref[...].astype(F32)
        local_states(cgr, False)
        send_states(1)

    def key_value():
        carry_in(False)
        add_carry(False, mix)
        kg_buf[...] = (mix[...] * v_ref[...].astype(F32)).astype(BF16)
        put(1, kg_buf, kg_ref).start()
        vg_buf[...] = (mix[...] * k_ref[...].astype(F32)).astype(BF16)
        put(2, vg_buf, vg_ref).start()

    def mixed_done():
        reduce_last()
        put(3, mixed_buf, mixed_ref).start()

    def weight_product(rows, first):
        total = lax.dot_general(
            gat[:, :, rows].reshape(N * half, C), cot_t[:, :, rows].reshape(N * half, C),
            (((0,), (0,)), ((), ())), preferred_element_type=F32,
        )
        if first:
            wacc[...] = total
        else:
            wg_buf[...] = (wacc[...] + total).astype(BF16)
            put(4, wg_buf, wg_ref).start()

    def put(n, buffer, out):
        return pltpu.make_async_copy(buffer, out, out_sem.at[n])

    def drain():
        drain_states(0)
        drain_states(1)
        for way in range(2):
            for phase, make in ((1, g1_copy), (2, g2_copy)):
                for part_at in range(2):
                    for hop in range(1, hops_of(phase, part_at) + 1):
                        make(part_at, way, hop, True).wait_send()

        for hop in range(1, H + 1):
            for way, k in ag_pieces(hop):
                ag_copy(way, hop, k, True).wait_send()
        for way, step, k in reduce_pieces():
            rr_copy(way, step, k).wait_send()

        @pl.loop(0, Z)
        def _(zz):
            cs_copy(zz, True).wait_send()
            sb_copy(zz, True).wait_send()

            @pl.when(zz * 2 + r != c)
            def _():
                aa_copy(zz).wait_send()

        pl.when(active)(lambda: others(N, c, drain_one))
        buffers = ((qg_buf, qg_ref), (kg_buf, kg_ref), (vg_buf, vg_ref), (mixed_buf, mixed_ref), (wg_buf, wg_ref))
        for n, (buffer, out) in enumerate(buffers):
            put(n, buffer, out).wait()

    top = max(X // 2, Y // 2)

    def arrive(hop, k):
        if hop < H:
            ag_arrive(hop, k)

    def gather_on(phase, lo, last=False):
        for hop in range(lo, top + 1):
            gather_wait(phase, hop) if last else gather_send(phase, hop)

    assert H <= 4
    near = list(range(-min(2, H - 1), min(2, H - 1) + 1))
    far = [away for away in range(-H + 1, H + 1) if away not in near]
    def scatter_at(away):
        if away <= H:
            scatter(away, away + 1)
            if away < H:
                scatter(-away, -away + 1)

    def projects(lo, hi):
        return lambda: project(min(lo, Z), min(hi, Z))

    steps = [
        ("begin", begin),
        ("barrier", lambda: pl.semaphore_wait(barrier, N - 1 + 3)),
        ("first_sends", first_sends),
        ("weights", spread_weights),
        ("taps", filter_taps),
        ("spectrum", filter_spectrum_loaded),
        ("send_rows", lambda: send_rows(0)),
        ("arrive1a", lambda: arrive(1, 0)),
        ("convolve", lambda: convolve(src, True, conv)),
        ("arrive1b", lambda: arrive(1, 1)),
        ("wait_rows", lambda: wait_rows(0)),
        ("gate", gate),
        ("scatter1", lambda: scatter(-min(1, H - 1), min(1, H - 1) + 1)),
        ("arrive2a", lambda: arrive(2, 0)),
        ("wait_weights", wait_weights),
        ("project_1", projects(0, 3)),
        ("arrive2b", lambda: arrive(2, 1)),
        ("reduce_first", reduce_first),
        ("scatter2", lambda: scatter_at(2) if H > 2 else None),
        ("project_2", projects(3, 5)),
        ("arrive3a", lambda: arrive(3, 0)),
        ("gather1_wait1", lambda: gather_wait(1, 1)),
        ("gather1_send2", lambda: gather_on(1, 2)),
        ("project_3", projects(5, Z)),
        ("arrive3b", lambda: arrive(3, 1)),
        ("reduce_second", reduce_second),
        ("scatter3", lambda: scatter_at(3) if H > 3 else None),
        ("gather1_wait2", lambda: gather_on(1, 2, True)),
        ("gather2_send1", lambda: gather_send(2, 1)),
        ("sibling_near", lambda: sibling_here(near)),
        ("back_near", lambda: multiply_back(near, True)),
        ("arrive_last", lambda: (ag_arrive(H, 0), ag_arrive(H, 1))),
        ("scatter_last", lambda: scatter_at(H)),
        ("reduce2a", lambda: reduce_step(2, 0)),
        ("sibling_far", lambda: sibling_here(far)),
        ("back_far", lambda: multiply_back(far)),
        ("reduce2b", lambda: reduce_step(2, 1)),
        ("back_states", back_states),
        ("correlate", lambda: convolve(cgr, False, mix)),
        ("pass_on", pass_on),
        ("reduce3a", lambda: reduce_step(3, 0)),
        ("gather2_wait1", lambda: gather_wait(2, 1)),
        ("gather2_send2", lambda: gather_on(2, 2)),
        ("reduce3b", lambda: reduce_step(3, 1)),
        ("send_back_rows", lambda: send_rows(1)),
        ("hand_over", hand_over),
        ("wait_back_rows", lambda: wait_rows(1)),
        ("key_value", key_value),
        ("handed_own", handed_own),
        ("gather2_wait2", lambda: gather_on(2, 2, True)),
        ("weight_own", lambda: weight_product(own_rows, True)),
        ("mixed_done", mixed_done),
        ("handed_over", handed_over),
        ("weight_other", lambda: weight_product(other_rows, False)),
        ("drain", drain),
    ]
    for name, step in steps:
        step()


def transforms(R):
    angle = np.pi / (2 * R) * (np.outer(2 * np.arange(R) + 1, np.arange(R)) % (4 * R))
    there = np.concatenate([np.cos(angle), -np.sin(angle)])
    result = []
    for table in (there, there.T / R):
        high = table.astype(np.float32).astype(ml_dtypes.bfloat16)
        low = (table - high.astype(np.float64)).astype(ml_dtypes.bfloat16)
        result.append(jnp.asarray(np.concatenate([high, low, high], axis=1)))
    return result


def finish(*refs):
    count = len(refs) // 3
    given, made, held = refs[:count], refs[count : 2 * count], refs[2 * count : 3 * count]
    in_sem, out_sem = refs[3 * count :]
    ins = [pltpu.make_async_copy(a, b, in_sem.at[n]) for n, (a, b) in enumerate(zip(given, held))]
    outs = [pltpu.make_async_copy(a, b, out_sem.at[n]) for n, (a, b) in enumerate(zip(held, made))]
    for one in ins:
        one.start()
    for one, other in zip(ins, outs):
        one.wait()
        other.start()
    for one in outs:
        one.wait()


def solution(mesh):
    N = mesh.shape["context"]
    X = math.isqrt(N)
    Y = N // X
    Z = mesh.shape["tensor"] // 2
    H = Z // 2

    def shards(query_rows, key_rows, value_rows, residue, decay_rate, out_weight, cotangent):
        R, C = query_rows.shape
        M = residue.shape[0]
        small = jax.ShapeDtypeStruct((R, C), BF16)
        dma = pltpu.SemaphoreType.DMA
        top = max(X // 2, Y // 2)
        anywhere = pl.BlockSpec(memory_space=pl.ANY)
        results = (small, small, small, small, jax.ShapeDtypeStruct((C, C), BF16))
        made = pl.pallas_call(
            functools.partial(body, X, Y, Z),
            out_shape=results,
            in_specs=[anywhere] * 9,
            out_specs=(anywhere,) * 5,
            scratch_shapes=[
                pltpu.VMEM((2 * Z, C, C), BF16),
                pltpu.VMEM((2 * Z, R, C), BF16),
                pltpu.VMEM((X, Y, R, C), BF16),
                pltpu.VMEM((X, Y, R, C), BF16),
                pltpu.VMEM((2 * Z, R, C), BF16),
                pltpu.VMEM((Z, R, C), BF16),
                pltpu.VMEM((2, H, R, C), BF16),
                pltpu.VMEM((2, H, R, C), BF16),
                pltpu.VMEM((2, Y, M, C), F32),
                pltpu.VMEM((2, X, M, C), F32),
                pltpu.VMEM((R, C), BF16),
                pltpu.VMEM((R, C), BF16),
                pltpu.VMEM((R, C), BF16),
                pltpu.VMEM((M, C), F32),
                pltpu.VMEM((M, C), F32),
                pltpu.VMEM((2 * R, 3 * R), BF16),
                pltpu.VMEM((R, 6 * R), BF16),
                dma((8,)),
                pltpu.VMEM((R, C), F32),
                pltpu.VMEM((R, C), F32),
                pltpu.VMEM((R, C), F32),
                pltpu.VMEM((R, C), F32),
                pltpu.VMEM((R, C), F32),
                pltpu.VMEM((R, C), F32),
                pltpu.VMEM((2 * R, C), F32),
                pltpu.VMEM((C, C), F32),
                pltpu.VMEM((M, 8, C), F32),
                pltpu.VMEM((M, 8, C), F32),
                pltpu.VMEM((M, 8, C), F32),
                pltpu.VMEM((M, 8, C), F32),
                pltpu.VMEM((R, C), BF16),
                pltpu.VMEM((R, C), BF16),
                pltpu.VMEM((R, C), BF16),
                pltpu.VMEM((R, C), BF16),
                pltpu.VMEM((C, C), BF16),
                dma((5,)),
                dma((2 * Z,)),
                dma((2, H, 2)),
                dma((2, H, 2)),
                dma((Z,)),
                dma((Z,)),
                dma((Z,)),
                dma((N,)),
                dma((2, N)),
                dma((2, N)),
                dma((2, N)),
                dma((2, N)),
                dma((2, Y)),
                dma((2, Y)),
                dma((2, X)),
                dma((2, X)),
                dma((2, 2, top)),
                dma((2, 2, top)),
                dma((2, 2, top)),
                dma((2, 2, top)),
                dma((Z,)),
                dma((Z,)),
                dma((2, H, 2)),
                dma((2, H, 2)),
            ],
            compiler_params=pltpu.CompilerParams(
                collective_id=0, has_side_effects=True, vmem_limit_bytes=56 * 1024 * 1024
            ),
            name="hyena_block",
        )(query_rows, key_rows, value_rows, residue, decay_rate, out_weight, cotangent, *transforms(R))
        return pl.pallas_call(
            finish,
            out_shape=results,
            in_specs=[anywhere] * 5,
            out_specs=(anywhere,) * 5,
            scratch_shapes=[pltpu.VMEM(one.shape, BF16) for one in results] + [dma((5,)), dma((5,))],
            compiler_params=pltpu.CompilerParams(vmem_limit_bytes=56 * 1024 * 1024),
            name="hand_out",
        )(*made)

    placed = (
        P("context", "tensor"),
        P("context", "tensor"),
        P("context", "tensor"),
        P(None, "tensor"),
        P(None, "tensor"),
        P("tensor", None),
        P("context", "tensor"),
    )
    return jax.shard_map(
        shards,
        mesh=mesh,
        in_specs=placed,
        out_specs=(
            P("context", "tensor"),
            P("context", "tensor"),
            P("context", "tensor"),
            P("context", "tensor"),
            P("tensor", "context"),
        ),
        check_vma=False,
    )
```

```python
import functools
import math

import jax
import jax.numpy as jnp
import ml_dtypes
import numpy as np
from jax import lax
from jax.experimental import pallas as pl
from jax.experimental.pallas import tpu as pltpu
from jax.sharding import PartitionSpec as P

MESH = pl.DeviceIdType.MESH
F32 = jnp.float32
BF16 = jnp.bfloat16
LANES = 128


def body(
    X, Y, Z,
    q_in, k_in, v_in, res_in, dec_in, w_ref, cot_in, fold_in, unfold_in,
    mixed_ref, qg_ref, kg_ref, vg_ref, wg_ref,
    wv, cot_all, cot_t, gat, part, sib, rs_out, rs_in, states, row_states,
    q_ref, k_ref, v_ref, res_ref, dec_ref, fold, unfold, in_sem,
    src, cgr, conv, back, mix, taps, taps_hat, wacc, rates, weights, powers, starts,
    w_sem, ag_ss, ag_rs, cs_ss, cs_rs, aa_ss, aa_rs, fw_ss, fw_rs, ex_ss, ex_rs, st_ss, st_rs, ro_ss, ro_rs,
    ga_ss, g1_rs, g2_rs, sb_ss, sb_rs, rr_ss, rr_rs,
):
    N = X * Y
    R, C = q_in.shape
    M = dec_in.shape[0]
    T = R // 8
    G = C // LANES
    H = Z // 2
    c = lax.axis_index("context")
    j = lax.axis_index("tensor")
    z, r = j // 2, j % 2
    cx, cy = c // Y, c % Y
    other = z * 2 + 1 - r
    mine = (c, j)
    sibling = (c, other)
    zdev = [(c, ((z + 1) % Z) * 2 + r), (c, ((z + Z - 1) % Z) * 2 + r)]
    xdev = [(((cx + 1) % X) * Y + cy, j), (((cx + X - 1) % X) * Y + cy, j)]
    ydev = [(cx * Y + (cy + 1) % Y, j), (cx * Y + (cy + Y - 1) % Y, j)]

    def copy(source, target, send_sem, recv_sem, device):
        return pltpu.make_async_remote_copy(
            src_ref=source, dst_ref=target, send_sem=send_sem, recv_sem=recv_sem,
            device_id=device, device_id_type=MESH,
        )

    def arrived(sem, ref):
        copy(ref, ref, sem, sem, mine).wait_recv()

    def left(sem, ref):
        copy(ref, ref, sem, sem, mine).wait_send()

    def lanes_of(g):
        return pl.ds(pl.multiple_of(g * LANES, LANES), LANES)

    barrier = pltpu.get_barrier_semaphore()
    for device in zdev + [sibling]:
        pl.semaphore_signal(barrier, inc=1, device_id=device, device_id_type=MESH)

    @pl.loop(0, N)
    def _(p):
        @pl.when(p != c)
        def _():
            pl.semaphore_signal(barrier, inc=1, device_id=(p, j), device_id_type=MESH)

    loads = (
        (k_in, k_ref), (v_in, v_ref), (dec_in, dec_ref), (cot_in, cot_all.at[j]), (res_in, res_ref),
        (fold_in, fold), (q_in, q_ref), (unfold_in, unfold),
    )

    def load(n):
        return pltpu.make_async_copy(*loads[n], in_sem.at[n])

    for n in range(len(loads)):
        load(n).start()

    def w_copy(n):
        return pltpu.make_async_copy(
            w_ref.at[:, pl.ds(pl.multiple_of(n * C, LANES), C)], wv.at[n], w_sem.at[0]
        )

    @pl.loop(0, 2 * Z)
    def _(n):
        w_copy(n).start()

    rows8 = lax.broadcasted_iota(jnp.int32, (8, LANES), 0).astype(F32)

    def spread_weights():
        load(4).wait()
        weight = res_ref[...] * jnp.sqrt(dec_ref[...])
        for m in range(M):
            weights[m] = jnp.broadcast_to(weight[m : m + 1], (8, C))

    def spread_rates():
        for m in range(M):
            rate = jnp.broadcast_to(dec_ref[pl.ds(m, 1), :], (8, C))
            rates[m] = rate
            powers[m] = jnp.exp(-8.0 * rate)

    def local_states(values, forward):
        way = 0 if forward else 1

        @pl.loop(0, G)
        def _(g):
            lanes = lanes_of(g)
            tiles = [values[pl.ds(8 * a, 8), lanes] for a in range(T)]
            if not forward:
                tiles = tiles[::-1]

            @pl.loop(0, M // 8)
            def _(eight):
                sums = []
                for inner in range(8):
                    m = eight * 8 + inner
                    step = powers[m, :, lanes]
                    total = tiles[0]
                    for tile in tiles[1:]:
                        total = total * step + tile
                    reach = 7.0 - rows8 if forward else rows8
                    total = total * jnp.exp(-rates[m, :, lanes] * reach)
                    sums.append(jnp.sum(total, axis=0, keepdims=True))
                modes = pl.ds(pl.multiple_of(eight * 8, 8), 8)
                states[way, cy, modes, lanes] = jnp.concatenate(sums, axis=0)

    def filter_taps():
        @pl.loop(0, G)
        def _(g):
            lanes = lanes_of(g)

            def add_mode(m, tiles):
                step = powers[m, :, lanes]
                term = weights[m, :, lanes] * jnp.exp(-rates[m, :, lanes] * rows8)
                new = []
                for a in range(T):
                    new.append(tiles[a] + term)
                    term = term * step
                return tuple(new)

            zero = jnp.zeros((8, LANES), F32)
            tiles = lax.fori_loop(0, M, add_mode, (zero,) * T, unroll=4)
            for a in range(T):
                taps[pl.ds(8 * a, 8), lanes] = tiles[a]

    width = min(C, 256)

    def halves(value):
        high = value.astype(BF16)
        return high, (value - high.astype(F32)).astype(BF16)

    def analyse(value):
        high, low = halves(value)
        return jnp.dot(fold[...], jnp.concatenate([high, high, low]), preferred_element_type=F32)

    def filter_spectrum():
        for lo in range(0, C, width):
            lanes = slice(lo, lo + width)
            taps_hat[:, lanes] = analyse(taps[:, lanes])

    def convolve(values, forward, out):
        for lo in range(0, C, width):
            lanes = slice(lo, lo + width)
            both = analyse(values[:, lanes])
            real, imag = both[:R], both[R:]
            tap_real, tap_imag = taps_hat[:R, lanes], taps_hat[R:, lanes]
            if forward:
                new_real = tap_real * real - tap_imag * imag
                new_imag = tap_real * imag + tap_imag * real
            else:
                new_real = tap_real * real + tap_imag * imag
                new_imag = tap_real * imag - tap_imag * real
            real_high, real_low = halves(new_real)
            imag_high, imag_low = halves(new_imag)
            out[:, lanes] = jnp.dot(
                unfold[...],
                jnp.concatenate([real_high, imag_high, real_high, imag_high, real_low, imag_low]),
                preferred_element_type=F32,
            )

    def carry_in(forward):
        way = 0 if forward else 1
        decay = jnp.exp(-float(R) * dec_ref[...])
        row_decay = jnp.exp(-float(R * Y) * dec_ref[...])

        def add_row(n, total):
            return total * row_decay + row_states[way, n if forward else X - 1 - n]

        def add_block(n, total):
            return total * decay + states[way, n if forward else Y - 1 - n]

        total = lax.fori_loop(0, cx if forward else X - 1 - cx, add_row, jnp.zeros((M, C), F32))
        total = lax.fori_loop(0, cy if forward else Y - 1 - cy, add_block, total)
        for m in range(M):
            starts[m] = weights[m] * total[m : m + 1]

    def add_carry(forward, out):
        @pl.loop(0, G)
        def _(g):
            lanes = lanes_of(g)

            def add_mode(m, tiles):
                rate, step = rates[m, :, lanes], powers[m, :, lanes]
                term = starts[m, :, lanes] * jnp.exp(-rate * ((rows8 + 1.0) if forward else (8.0 - rows8)))
                new = []
                for a in range(T):
                    new.append(tiles[a] + term)
                    term = term * step
                return tuple(new)

            order = list(range(T)) if forward else list(range(T))[::-1]
            tiles = lax.fori_loop(
                0, M, add_mode, tuple(out[pl.ds(8 * a, 8), lanes] for a in order), unroll=4
            )
            for n, a in enumerate(order):
                out[pl.ds(8 * a, 8), lanes] = tiles[n]

    def state_copy(way, y, sending):
        ref = states.at[way, cy if sending else y]
        sem = st_rs.at[way]
        return copy(ref, ref, st_ss.at[way], sem, (cx * Y + y, j))

    def row_copy(way, x, sending):
        ref = row_states.at[way, cx if sending else x]
        sem = ro_rs.at[way]
        return copy(ref, ref, ro_ss.at[way], sem, (x * Y + cy, j))

    def others(count, here, act):
        @pl.loop(0, count)
        def _(n):
            pl.when(n != here)(lambda: act(n))

    def send_states(way):
        others(Y, cy, lambda y: state_copy(way, y, True).start())

    def send_rows(way):
        arrived(st_rs.at[way], states.at[way, pl.ds(0, Y - 1)])
        decay = jnp.exp(-float(R) * dec_ref[...])
        order = range(Y) if way == 0 else range(Y)[::-1]
        total = states[way, order[0]]
        for y in order[1:]:
            total = total * decay + states[way, y]
        row_states[way, cx] = total

        others(X, cx, lambda x: row_copy(way, x, True).start())

    def wait_rows(way):
        arrived(ro_rs.at[way], row_states.at[way, pl.ds(0, X - 1)])

    def drain_states(way):
        left(st_ss.at[way], states.at[way, pl.ds(0, Y - 1)])
        left(ro_ss.at[way], row_states.at[way, pl.ds(0, X - 1)])

    near = list(range(-min(2, H - 1), min(2, H - 1) + 1))
    far = [away for away in range(-H + 1, H + 1) if away not in near]

    def piece(way, hop, last, size):
        if hop < last:
            return pl.ds(0, size)
        return pl.ds(way * (size // 2), size // 2)

    def ag_copy(way, hop, k, sending):
        away = hop - 1 if sending else hop
        owner = (z - away + Z) % Z if way == 0 else (z + away) % Z
        ref = cot_all.at[owner * 2 + r, pl.ds(k * (R // 2), R // 2)]
        return copy(ref, ref, ag_ss.at[0], ag_rs.at[way, hop - 1, k], zdev[way])

    def ag_pieces(hop):
        return [(way, k) for k in range(2) for way in range(2) if hop < H or way == k]

    def spread(away):
        ref = cot_all.at[(z + Z + away) % Z * 2 + r]
        group = 0 if away in near else 1
        copy(ref, ref, cs_ss.at[0], cs_rs.at[group], sibling).start()

    def sibling_here(group):
        arrived(cs_rs.at[group], cot_all.at[pl.ds(0, len((near, far)[group]))])

    odd = z % 2
    own_rows = pl.ds(pl.multiple_of(odd * (R // 2), R // 2), R // 2)
    other_rows = pl.ds(pl.multiple_of((1 - odd) * (R // 2), R // 2), R // 2)

    def aa_copy(zz):
        owner = zz * 2 + r
        return copy(
            cot_all.at[owner, own_rows], cot_t.at[c, own_rows], aa_ss.at[0], aa_rs.at[cx], (owner, j)
        )

    def scatter(lo, hi):
        count = hi - lo

        @pl.loop(0, count)
        def _(n):
            zz = (z + Z + lo + (c // 2 + n) % count) % Z

            @pl.when(zz * 2 + r != c)
            def _():
                aa_copy(zz).start()

    def ag_start():
        for way, k in ag_pieces(1):
            ag_copy(way, 1, k, True).start()

    def ag_arrive(hop, half_at):
        for way, k in ag_pieces(hop):
            if k == half_at:
                ag_copy(way, hop, k, False).wait_recv()
                if (way, k) in ag_pieces(hop + 1) and hop < H:
                    ag_copy(way, hop + 1, k, True).start()
        if half_at == 1:
            spread(hop)
            if hop < H:
                spread(-hop)

    half = R // 2

    def g1_copy(part_at, way, hop, sending):
        size, last, devices, at = (X, X // 2, xdev, cx) if part_at == 0 else (Y, Y // 2, ydev, cy)
        away = hop - 1 if sending else hop
        owner = (at - away + size) % size if way == 0 else (at + away) % size
        low = part_at * half
        if hop == last:
            rows = pl.ds(low + way * (half // 2), half // 2)
        else:
            rows = pl.ds(low, half)
        ref = gat.at[owner, cy, rows] if part_at == 0 else gat.at[cx, owner, rows]
        return copy(ref, ref, ga_ss.at[0], g1_rs.at[hop - 1], devices[way])

    def g2_copy(part_at, way, hop, sending):
        size, last, devices, at, many = (
            (Y, Y // 2, ydev, cy, X) if part_at == 0 else (X, X // 2, xdev, cx, Y)
        )
        away = hop - 1 if sending else hop
        owner = (at - away + size) % size if way == 0 else (at + away) % size
        group = piece(way, hop, last, many)
        rows = pl.ds(part_at * half, half)
        ref = gat.at[group, owner, rows] if part_at == 0 else gat.at[owner, group, rows]
        return copy(ref, ref, ga_ss.at[0], g2_rs.at[hop - 1], devices[way])

    def hops_of(phase, part_at):
        return (X // 2, Y // 2)[part_at if phase == 1 else 1 - part_at]

    def gather_send(phase, hop):
        make = g1_copy if phase == 1 else g2_copy
        for part_at in range(2):
            if hop <= hops_of(phase, part_at):
                for way in range(2):
                    make(part_at, way, hop, True).start()

    def gather_wait(phase, hop):
        count = 2 if hop < X // 2 else 1
        if phase == 1:
            arrived(g1_rs.at[hop - 1], gat.at[0, pl.ds(0, count)])
        else:
            arrived(g2_rs.at[hop - 1], gat.at[pl.ds(0, count)])

    def sb_copy(zz, sending):
        target = zz * 2 + (1 - r if sending else r)
        return copy(part.at[target], sib.at[zz], sb_ss.at[0], sb_rs.at[zz], sibling)

    def project(lo, hi):
        @pl.loop(lo, hi)
        def _(o):
            hop = H - (o + 1) // 2
            zz = (z + Z + hop * (2 * (o % 2) - 1)) % Z
            gated = gat[cx, cy]
            for core in range(2):
                target = zz * 2 + ((1 - r) if core == 0 else r)
                part[target] = jnp.dot(
                    gated, wv[target], preferred_element_type=F32
                ).astype(BF16)
                if core == 0:
                    sb_copy(zz, True).start()

    halves_of = (pl.ds(0, half), pl.ds(half, half))

    def rr_copy(way, step, k):
        return copy(
            rs_out.at[way, step, halves_of[k]], rs_in.at[way, step, halves_of[k]],
            rr_ss.at[0], rr_rs.at[way, step, k], zdev[way],
        )

    def pair_sum(zz, k):
        return part[zz * 2 + r, halves_of[k]].astype(F32) + sib[zz, halves_of[k]].astype(F32)

    def reduce_target(way, step):
        away = H - step
        return (z + away) % Z if way == 0 else (z - away + Z) % Z

    def reduce_piece(way, step, k, arrived):
        total = pair_sum(reduce_target(way, step), k)
        if arrived:
            rr_copy(way, step - 1, k).wait_recv()
            total = total + rs_in[way, step - 1, halves_of[k]].astype(F32)
        rs_out[way, step, halves_of[k]] = total.astype(BF16)
        rr_copy(way, step, k).start()

    def reduce_first():
        sb_copy((z + H) % Z, False).wait_recv()
        for way in range(2):
            reduce_piece(way, 0, way, False)
        if H > 1:
            for way in range(2):
                sb_copy(reduce_target(way, 1), False).wait_recv()
                reduce_piece(way, 1, 1 - way, False)

    def reduce_second():
        if H > 1:
            for way in range(2):
                reduce_piece(way, 1, way, True)

    def reduce_step(step, k):
        if step < H:
            for way in range(2):
                if k == 0:
                    sb_copy(reduce_target(way, step), False).wait_recv()
                reduce_piece(way, step, k, True)

    def reduce_last():
        sb_copy(z, False).wait_recv()
        for k in range(2):
            total = pair_sum(z, k)
            for way in range(2):
                if H > 1 or way == k:
                    rr_copy(way, H - 1, k).wait_recv()
                    total = total + rs_in[way, H - 1, halves_of[k]].astype(F32)
            mixed_ref[halves_of[k]] = total.astype(BF16)

    active = c % 2 == r

    def fw_copy(own, n):
        ref = cot_t.at[pl.ds(n * Y, Y), own_rows if own else other_rows]
        return copy(ref, ref, fw_ss.at[0], fw_rs.at[0 if own else 1], sibling)

    def ex_copy(way, n, sending):
        side = odd if sending else 1 - odd
        low = pl.multiple_of(side * (R // 2) + way * (R // 4), R // 4)
        ref = cot_t.at[pl.ds(n * Y, Y), pl.ds(low, R // 4)]
        return copy(ref, ref, ex_ss.at[0], ex_rs.at[way, n], zdev[way])

    def group_arrived(n):
        def some(count):
            return lambda: arrived(aa_rs.at[n], cot_t.at[pl.ds(0, count), pl.ds(0, R // 2)])

        pl.when(n == cx)(some(Y - 1))
        pl.when(n != cx)(some(Y))

    def pass_group(n):
        group_arrived(n)
        for way in range(2):
            ex_copy(way, n, True).start()
        fw_copy(True, n).start()

    reach = (z - c // 2 + Z) % Z

    def pass_on(*distances):
        chosen = [reach == away % Z for away in set(distances) | {-away for away in distances}]

        @pl.when(jnp.logical_and(active, functools.reduce(jnp.logical_or, chosen)))
        def _():
            cot_t[c, own_rows] = cot_all[c, own_rows]
            pl.loop(0, X)(pass_group)

    def hand_group(n):
        for way in range(2):
            ex_copy(way, n, False).wait_recv()
        fw_copy(False, n).start()

    def hand_over():
        pl.when(active)(lambda: pl.loop(0, X)(hand_group))

    def handed(own):
        rows = pl.ds(0, R // 2)
        pl.when(jnp.logical_not(active))(lambda: arrived(fw_rs.at[0 if own else 1], cot_t.at[:, rows]))

    def drain_passed():
        @pl.when(active)
        def _():
            left(ex_ss.at[0], cot_t.at[:, pl.ds(0, R // 2)])
            left(fw_ss.at[0], cot_t)
            left(aa_ss.at[0], cot_t.at[pl.ds(0, Z - 1), pl.ds(0, R // 2)])

        @pl.when(jnp.logical_not(active))
        def _():
            left(aa_ss.at[0], cot_t.at[pl.ds(0, Z), pl.ds(0, R // 2)])

    def wait_weights():
        pltpu.make_async_copy(wv, wv, w_sem.at[0]).wait()

    def begin():
        for n in (0, 1, 2):
            load(n).wait()
        src[...] = k_ref[...].astype(F32) * v_ref[...].astype(F32)
        spread_rates()
        local_states(src, True)

    def first_sends():
        load(3).wait()
        send_states(0)
        ag_start()
        spread(0)

    def filter_spectrum_loaded():
        for n in (5, 6, 7):
            load(n).wait()
        filter_spectrum()

    def gate():
        carry_in(True)
        add_carry(True, conv)
        gat[cx, cy] = (q_ref[...].astype(F32) * conv[...]).astype(BF16)
        gather_send(1, 1)

    def multiply_back(distances, cores, first=False):
        if not distances:
            return
        zs = [(z + Z + away) % Z for away in distances]
        blocks = [zz * 2 + core for zz in zs for core in cores]
        total = lax.dot_general(
            jnp.concatenate([cot_all[n] for n in blocks], axis=1),
            jnp.concatenate([wv[n] for n in blocks], axis=1),
            (((1,), (1,)), ((), ())), preferred_element_type=F32,
        )
        back[...] = total if first else back[...] + total

    def back_states():
        qg_ref[...] = (back[...] * conv[...]).astype(BF16)
        cgr[...] = back[...] * q_ref[...].astype(F32)
        local_states(cgr, False)
        send_states(1)

    def key_value():
        carry_in(False)
        add_carry(False, mix)
        kg_ref[...] = (mix[...] * v_ref[...].astype(F32)).astype(BF16)
        vg_ref[...] = (mix[...] * k_ref[...].astype(F32)).astype(BF16)

    def mixed_done():
        reduce_last()

    def weight_product(rows, first):
        total = lax.dot_general(
            gat[:, :, rows].reshape(N * half, C), cot_t[:, rows].reshape(N * half, C),
            (((0,), (0,)), ((), ())), preferred_element_type=F32,
        )
        if first:
            wacc[...] = total
        else:
            wg_ref[...] = (wacc[...] + total).astype(BF16)

    def drain():
        drain_states(0)
        drain_states(1)
        left(ag_ss.at[0], cot_all.at[pl.ds(0, Z - 1)])
        left(cs_ss.at[0], cot_all.at[pl.ds(0, Z)])
        left(sb_ss.at[0], sib)
        left(rr_ss.at[0], cot_all.at[pl.ds(0, Z - 1)])
        left(ga_ss.at[0], cot_all.at[pl.ds(0, N - 1)])
        drain_passed()

    top = max(X // 2, Y // 2)

    def arrive(hop, k):
        if hop < H:
            ag_arrive(hop, k)

    def gather_on(phase, lo, last=False):
        for hop in range(lo, top + 1):
            gather_wait(phase, hop) if last else gather_send(phase, hop)

    assert H <= 4 and X == Y and N == 2 * Z
    def scatter_at(away):
        if away <= H:
            scatter(away, away + 1)
            if away < H:
                scatter(-away, -away + 1)

    def projects(lo, hi):
        return lambda: project(min(lo, Z), min(hi, Z))

    same, both = (r,), (0, 1)
    steps = [
        ("begin", begin),
        ("barrier", lambda: pl.semaphore_wait(barrier, N - 1 + 3)),
        ("first_sends", first_sends),
        ("weights", spread_weights),
        ("taps", filter_taps),
        ("spectrum", filter_spectrum_loaded),
        ("send_rows", lambda: send_rows(0)),
        ("arrive1a", lambda: arrive(1, 0)),
        ("convolve", lambda: convolve(src, True, conv)),
        ("arrive1b", lambda: arrive(1, 1)),
        ("wait_rows", lambda: wait_rows(0)),
        ("gate", gate),
        ("scatter01", lambda: scatter(-min(1, H - 1), min(1, H - 1) + 1)),
        ("arrive2a", lambda: arrive(2, 0)),
        ("wait_weights", wait_weights),
        ("project_1", projects(0, 3)),
        ("arrive2b", lambda: arrive(2, 1)),
        ("scatter2", lambda: scatter_at(2) if H > 2 else None),
        ("project_2", projects(3, 5)),
        ("arrive3a", lambda: arrive(3, 0)),
        ("project_3", projects(5, Z)),
        ("arrive3b", lambda: arrive(3, 1)),
        ("reduce_first", reduce_first),
        ("scatter3", lambda: scatter_at(3) if H > 3 else None),
        ("gather1_wait1", lambda: gather_wait(1, 1)),
        ("gather1_send2", lambda: gather_on(1, 2)),
        ("sibling_near", lambda: sibling_here(0)),
        ("back_near", lambda: multiply_back(near, both, True)),
        ("pass_0", lambda: pass_on(0)),
        ("arrive_last", lambda: (ag_arrive(H, 0), ag_arrive(H, 1))),
        ("scatter_last", lambda: scatter_at(H)),
        ("reduce_second", reduce_second),
        ("back_far_same", lambda: multiply_back(far, same)),
        ("pass_1", lambda: pass_on(1) if H > 1 else None),
        ("gather1_wait2", lambda: gather_on(1, 2, True)),
        ("gather2_send1", lambda: gather_send(2, 1)),
        ("pass_2", lambda: pass_on(2) if H > 2 else None),
        ("sibling_far", lambda: sibling_here(1)),
        ("back_far_other", lambda: multiply_back(far, (1 - r,))),
        ("back_states", back_states),
        ("reduce2a", lambda: reduce_step(2, 0)),
        ("correlate", lambda: convolve(cgr, False, mix)),
        ("reduce2b", lambda: reduce_step(2, 1)),
        ("pass_3", lambda: pass_on(3) if H > 3 else None),
        ("pass_last", lambda: pass_on(H)),
        ("send_back_rows", lambda: send_rows(1)),
        ("gather2_wait1", lambda: gather_wait(2, 1)),
        ("gather2_send2", lambda: gather_on(2, 2)),
        ("reduce3a", lambda: reduce_step(3, 0)),
        ("reduce3b", lambda: reduce_step(3, 1)),
        ("hand_over", hand_over),
        ("wait_back_rows", lambda: wait_rows(1)),
        ("key_value", key_value),
        ("handed_own", lambda: handed(True)),
        ("gather2_wait2", lambda: gather_on(2, 2, True)),
        ("weight_own", lambda: weight_product(own_rows, True)),
        ("mixed_done", mixed_done),
        ("handed_over", lambda: handed(False)),
        ("weight_other", lambda: weight_product(other_rows, False)),
        ("drain", drain),
    ]
    for name, step in steps:
        step()


def transforms(R):
    angle = np.pi / (2 * R) * (np.outer(2 * np.arange(R) + 1, np.arange(R)) % (4 * R))
    there = np.concatenate([np.cos(angle), -np.sin(angle)])
    result = []
    for table in (there, there.T / R):
        high = table.astype(np.float32).astype(ml_dtypes.bfloat16)
        low = (table - high.astype(np.float64)).astype(ml_dtypes.bfloat16)
        result.append(jnp.asarray(np.concatenate([high, low, high], axis=1)))
    return result


def finish(*refs):
    count = len(refs) // 2
    given, made, sem = refs[:count], refs[count : 2 * count], refs[-1]
    copies = [pltpu.make_async_copy(a, b, sem.at[n]) for n, (a, b) in enumerate(zip(given, made))]
    for one in copies:
        one.start()
    for one in copies:
        one.wait()


def solution(mesh):
    N = mesh.shape["context"]
    X = math.isqrt(N)
    Y = N // X
    Z = mesh.shape["tensor"] // 2
    H = Z // 2

    def shards(query_rows, key_rows, value_rows, residue, decay_rate, out_weight, cotangent):
        R, C = query_rows.shape
        M = residue.shape[0]
        small = jax.ShapeDtypeStruct((R, C), BF16)
        dma = pltpu.SemaphoreType.DMA
        top = max(X // 2, Y // 2)
        anywhere = pl.BlockSpec(memory_space=pl.ANY)
        results = (small, small, small, small, jax.ShapeDtypeStruct((C, C), BF16))
        made = pl.pallas_call(
            functools.partial(body, X, Y, Z),
            out_shape=tuple(pltpu.VMEM(one.shape, BF16) for one in results),
            in_specs=[anywhere] * 9,
            out_specs=(pl.BlockSpec(memory_space=pltpu.VMEM),) * 5,
            scratch_shapes=[
                pltpu.VMEM((2 * Z, C, C), BF16),
                pltpu.VMEM((2 * Z, R, C), BF16),
                pltpu.VMEM((N, R, C), BF16),
                pltpu.VMEM((X, Y, R, C), BF16),
                pltpu.VMEM((2 * Z, R, C), BF16),
                pltpu.VMEM((Z, R, C), BF16),
                pltpu.VMEM((2, H, R, C), BF16),
                pltpu.VMEM((2, H, R, C), BF16),
                pltpu.VMEM((2, Y, M, C), F32),
                pltpu.VMEM((2, X, M, C), F32),
                pltpu.VMEM((R, C), BF16),
                pltpu.VMEM((R, C), BF16),
                pltpu.VMEM((R, C), BF16),
                pltpu.VMEM((M, C), F32),
                pltpu.VMEM((M, C), F32),
                pltpu.VMEM((2 * R, 3 * R), BF16),
                pltpu.VMEM((R, 6 * R), BF16),
                dma((8,)),
                pltpu.VMEM((R, C), F32),
                pltpu.VMEM((R, C), F32),
                pltpu.VMEM((R, C), F32),
                pltpu.VMEM((R, C), F32),
                pltpu.VMEM((R, C), F32),
                pltpu.VMEM((R, C), F32),
                pltpu.VMEM((2 * R, C), F32),
                pltpu.VMEM((C, C), F32),
                pltpu.VMEM((M, 8, C), F32),
                pltpu.VMEM((M, 8, C), F32),
                pltpu.VMEM((M, 8, C), F32),
                pltpu.VMEM((M, 8, C), F32),
                dma((1,)),
                dma((1,)),
                dma((2, H, 2)),
                dma((1,)),
                dma((2,)),
                dma((1,)),
                dma((X,)),
                dma((1,)),
                dma((2,)),
                dma((1,)),
                dma((2, X)),
                dma((2,)),
                dma((2,)),
                dma((2,)),
                dma((2,)),
                dma((1,)),
                dma((top,)),
                dma((top,)),
                dma((1,)),
                dma((Z,)),
                dma((1,)),
                dma((2, H, 2)),
            ],
            compiler_params=pltpu.CompilerParams(
                collective_id=0, has_side_effects=True, vmem_limit_bytes=56 * 1024 * 1024
            ),
            name="hyena_block",
        )(query_rows, key_rows, value_rows, residue, decay_rate, out_weight, cotangent, *transforms(R))
        return pl.pallas_call(
            finish,
            out_shape=results,
            in_specs=[anywhere] * 5,
            out_specs=(anywhere,) * 5,
            scratch_shapes=[dma((5,))],
            compiler_params=pltpu.CompilerParams(vmem_limit_bytes=1024 * 1024),
            name="hand_out",
        )(*made)

    placed = (
        P("context", "tensor"),
        P("context", "tensor"),
        P("context", "tensor"),
        P(None, "tensor"),
        P(None, "tensor"),
        P("tensor", None),
        P("context", "tensor"),
    )
    return jax.shard_map(
        shards,
        mesh=mesh,
        in_specs=placed,
        out_specs=(
            P("context", "tensor"),
            P("context", "tensor"),
            P("context", "tensor"),
            P("context", "tensor"),
            P("tensor", "context"),
        ),
        check_vma=False,
    )
```

```python
import functools
import math

import jax
import jax.numpy as jnp
import ml_dtypes
import numpy as np
from jax import lax
from jax.experimental import pallas as pl
from jax.experimental.pallas import tpu as pltpu
from jax.sharding import PartitionSpec as P

MESH = pl.DeviceIdType.MESH
F32 = jnp.float32
BF16 = jnp.bfloat16
LANES = 128


def body(
    X, Y, Z,
    q_in, k_in, v_in, res_in, dec_in, w_ref, cot_in, fold_in, unfold_in,
    mixed_ref, qg_ref, kg_ref, vg_ref, wg_ref,
    wv, cot_all, cot_t, gat, part, sib, rs_out, rs_in, states, row_states,
    q_ref, k_ref, v_ref, res_ref, dec_ref, fold, unfold, in_sem,
    src, cgr, conv, back, mix, taps, taps_hat, wacc, rates, weights, powers, starts,
    w_sem, ag_ss, ag_rs, cs_ss, cs_rs, aa_ss, aa_rs, fw_ss, fw_rs, ex_ss, ex_rs, st_ss, st_rs, ro_ss, ro_rs,
    ga_ss, g1_rs, g2_rs, sb_ss, sb_rs, rr_ss, rr_rs,
):
    N = X * Y
    R, C = q_in.shape
    M = dec_in.shape[0]
    T = R // 8
    G = C // LANES
    H = Z // 2
    c = lax.axis_index("context")
    j = lax.axis_index("tensor")
    z, r = j // 2, j % 2
    cx, cy = c // Y, c % Y
    other = z * 2 + 1 - r
    mine = (c, j)
    sibling = (c, other)
    zdev = [(c, ((z + 1) % Z) * 2 + r), (c, ((z + Z - 1) % Z) * 2 + r)]
    xdev = [(((cx + 1) % X) * Y + cy, j), (((cx + X - 1) % X) * Y + cy, j)]
    ydev = [(cx * Y + (cy + 1) % Y, j), (cx * Y + (cy + Y - 1) % Y, j)]

    def copy(source, target, send_sem, recv_sem, device):
        return pltpu.make_async_remote_copy(
            src_ref=source, dst_ref=target, send_sem=send_sem, recv_sem=recv_sem,
            device_id=device, device_id_type=MESH,
        )

    def arrived(sem, ref):
        copy(ref, ref, sem, sem, mine).wait_recv()

    def left(sem, ref):
        copy(ref, ref, sem, sem, mine).wait_send()

    def lanes_of(g):
        return pl.ds(pl.multiple_of(g * LANES, LANES), LANES)

    barrier = pltpu.get_barrier_semaphore()
    for device in zdev + [sibling]:
        pl.semaphore_signal(barrier, inc=1, device_id=device, device_id_type=MESH)

    @pl.loop(0, N)
    def _(p):
        @pl.when(p != c)
        def _():
            pl.semaphore_signal(barrier, inc=1, device_id=(p, j), device_id_type=MESH)

    loads = (
        (k_in, k_ref), (v_in, v_ref), (dec_in, dec_ref), (cot_in, cot_all.at[j]), (res_in, res_ref),
        (fold_in, fold), (q_in, q_ref), (unfold_in, unfold),
    )

    def load(n):
        return pltpu.make_async_copy(*loads[n], in_sem.at[n])

    for n in range(len(loads)):
        load(n).start()

    def w_copy(n):
        return pltpu.make_async_copy(
            w_ref.at[:, pl.ds(pl.multiple_of(n * C, LANES), C)], wv.at[n], w_sem.at[0]
        )

    @pl.loop(0, 2 * Z)
    def _(n):
        w_copy(n).start()

    rows8 = lax.broadcasted_iota(jnp.int32, (8, LANES), 0).astype(F32)

    def spread_weights():
        load(4).wait()
        weight = res_ref[...] * jnp.sqrt(dec_ref[...])
        for m in range(M):
            weights[m] = jnp.broadcast_to(weight[m : m + 1], (8, C))

    def spread_rates():
        for m in range(M):
            rate = jnp.broadcast_to(dec_ref[pl.ds(m, 1), :], (8, C))
            rates[m] = rate
            powers[m] = jnp.exp(-8.0 * rate)

    def local_states(values, forward):
        way = 0 if forward else 1

        @pl.loop(0, G)
        def _(g):
            lanes = lanes_of(g)
            tiles = [values[pl.ds(8 * a, 8), lanes] for a in range(T)]
            if not forward:
                tiles = tiles[::-1]

            @pl.loop(0, M // 8)
            def _(eight):
                sums = []
                for inner in range(8):
                    m = eight * 8 + inner
                    step = powers[m, :, lanes]
                    total = tiles[0]
                    for tile in tiles[1:]:
                        total = total * step + tile
                    reach = 7.0 - rows8 if forward else rows8
                    total = total * jnp.exp(-rates[m, :, lanes] * reach)
                    sums.append(jnp.sum(total, axis=0, keepdims=True))
                modes = pl.ds(pl.multiple_of(eight * 8, 8), 8)
                states[way, cy, modes, lanes] = jnp.concatenate(sums, axis=0)

    def filter_taps():
        @pl.loop(0, G)
        def _(g):
            lanes = lanes_of(g)

            def add_mode(m, tiles):
                step = powers[m, :, lanes]
                term = weights[m, :, lanes] * jnp.exp(-rates[m, :, lanes] * rows8)
                new = []
                for a in range(T):
                    new.append(tiles[a] + term)
                    term = term * step
                return tuple(new)

            zero = jnp.zeros((8, LANES), F32)
            tiles = lax.fori_loop(0, M, add_mode, (zero,) * T, unroll=4)
            for a in range(T):
                taps[pl.ds(8 * a, 8), lanes] = tiles[a]

    width = min(C, 256)

    def halves(value):
        high = value.astype(BF16)
        return high, (value - high.astype(F32)).astype(BF16)

    def analyse(value):
        high, low = halves(value)
        return jnp.dot(fold[...], jnp.concatenate([high, high, low]), preferred_element_type=F32)

    def filter_spectrum():
        for lo in range(0, C, width):
            lanes = slice(lo, lo + width)
            taps_hat[:, lanes] = analyse(taps[:, lanes])

    def convolve(values, forward, out):
        for lo in range(0, C, width):
            lanes = slice(lo, lo + width)
            both = analyse(values[:, lanes])
            real, imag = both[:R], both[R:]
            tap_real, tap_imag = taps_hat[:R, lanes], taps_hat[R:, lanes]
            if forward:
                new_real = tap_real * real - tap_imag * imag
                new_imag = tap_real * imag + tap_imag * real
            else:
                new_real = tap_real * real + tap_imag * imag
                new_imag = tap_real * imag - tap_imag * real
            real_high, real_low = halves(new_real)
            imag_high, imag_low = halves(new_imag)
            out[:, lanes] = jnp.dot(
                unfold[...],
                jnp.concatenate([real_high, imag_high, real_high, imag_high, real_low, imag_low]),
                preferred_element_type=F32,
            )

    def carry_in(forward):
        way = 0 if forward else 1
        decay = jnp.exp(-float(R) * dec_ref[...])
        row_decay = jnp.exp(-float(R * Y) * dec_ref[...])

        def add_row(n, total):
            return total * row_decay + row_states[way, n if forward else X - 1 - n]

        def add_block(n, total):
            return total * decay + states[way, n if forward else Y - 1 - n]

        total = lax.fori_loop(0, cx if forward else X - 1 - cx, add_row, jnp.zeros((M, C), F32))
        total = lax.fori_loop(0, cy if forward else Y - 1 - cy, add_block, total)
        for m in range(M):
            starts[m] = weights[m] * total[m : m + 1]

    def add_carry(forward, out):
        @pl.loop(0, G)
        def _(g):
            lanes = lanes_of(g)

            def add_mode(m, tiles):
                rate, step = rates[m, :, lanes], powers[m, :, lanes]
                term = starts[m, :, lanes] * jnp.exp(-rate * ((rows8 + 1.0) if forward else (8.0 - rows8)))
                new = []
                for a in range(T):
                    new.append(tiles[a] + term)
                    term = term * step
                return tuple(new)

            order = list(range(T)) if forward else list(range(T))[::-1]
            tiles = lax.fori_loop(
                0, M, add_mode, tuple(out[pl.ds(8 * a, 8), lanes] for a in order), unroll=4
            )
            for n, a in enumerate(order):
                out[pl.ds(8 * a, 8), lanes] = tiles[n]

    def state_copy(way, y, sending):
        ref = states.at[way, cy if sending else y]
        sem = st_rs.at[way]
        return copy(ref, ref, st_ss.at[way], sem, (cx * Y + y, j))

    def row_copy(way, x, sending):
        ref = row_states.at[way, cx if sending else x]
        sem = ro_rs.at[way]
        return copy(ref, ref, ro_ss.at[way], sem, (x * Y + cy, j))

    def others(count, here, act):
        @pl.loop(0, count)
        def _(n):
            pl.when(n != here)(lambda: act(n))

    def send_states(way):
        others(Y, cy, lambda y: state_copy(way, y, True).start())

    def send_rows(way):
        arrived(st_rs.at[way], states.at[way, pl.ds(0, Y - 1)])
        decay = jnp.exp(-float(R) * dec_ref[...])
        order = range(Y) if way == 0 else range(Y)[::-1]
        total = states[way, order[0]]
        for y in order[1:]:
            total = total * decay + states[way, y]
        row_states[way, cx] = total

        others(X, cx, lambda x: row_copy(way, x, True).start())

    def wait_rows(way):
        arrived(ro_rs.at[way], row_states.at[way, pl.ds(0, X - 1)])

    def drain_states(way):
        left(st_ss.at[way], states.at[way, pl.ds(0, Y - 1)])
        left(ro_ss.at[way], row_states.at[way, pl.ds(0, X - 1)])

    near = list(range(-min(2, H - 1), min(2, H - 1) + 1))
    far = [away for away in range(-H + 1, H + 1) if away not in near]

    def piece(way, hop, last, size):
        if hop < last:
            return pl.ds(0, size)
        return pl.ds(way * (size // 2), size // 2)

    def ag_copy(way, hop, k, sending):
        away = hop - 1 if sending else hop
        owner = (z - away + Z) % Z if way == 0 else (z + away) % Z
        ref = cot_all.at[owner * 2 + r, pl.ds(k * (R // 2), R // 2)]
        return copy(ref, ref, ag_ss.at[0], ag_rs.at[way, hop - 1, k], zdev[way])

    def ag_pieces(hop):
        return [(way, k) for k in range(2) for way in range(2) if hop < H or way == k]

    def spread(away):
        ref = cot_all.at[(z + Z + away) % Z * 2 + r]
        group = 0 if away in near else 1
        copy(ref, ref, cs_ss.at[0], cs_rs.at[group], sibling).start()

    def sibling_here(group):
        arrived(cs_rs.at[group], cot_all.at[pl.ds(0, len((near, far)[group]))])

    odd = z % 2
    own_rows = pl.ds(pl.multiple_of(odd * (R // 2), R // 2), R // 2)
    other_rows = pl.ds(pl.multiple_of((1 - odd) * (R // 2), R // 2), R // 2)

    def aa_copy(zz):
        owner = zz * 2 + r
        return copy(
            cot_all.at[owner, own_rows], cot_t.at[c, own_rows], aa_ss.at[0], aa_rs.at[cx], (owner, j)
        )

    def scatter(lo, hi):
        count = hi - lo

        @pl.loop(0, count)
        def _(n):
            zz = (z + Z + lo + (c // 2 + n) % count) % Z

            @pl.when(zz * 2 + r != c)
            def _():
                aa_copy(zz).start()

    def ag_start():
        for way, k in ag_pieces(1):
            ag_copy(way, 1, k, True).start()

    def ag_arrive(hop, half_at):
        for way, k in ag_pieces(hop):
            if k == half_at:
                ag_copy(way, hop, k, False).wait_recv()
                if (way, k) in ag_pieces(hop + 1) and hop < H:
                    ag_copy(way, hop + 1, k, True).start()
        if half_at == 1:
            spread(hop)
            if hop < H:
                spread(-hop)

    half = R // 2

    def gather_first():
        for part_at in range(2):
            ref = gat.at[cx, cy, pl.ds(part_at * half, half)]
            for away in range(1, X):
                to = ((cx + away) % X) * Y + cy if part_at == 0 else cx * Y + (cy + away) % Y
                copy(ref, ref, ga_ss.at[0], g1_rs.at[0], (to, j)).start()

    def gather_first_here():
        arrived(g1_rs.at[0], gat.at[0, pl.ds(0, X - 1)])

    def g2_copy(part_at, way, hop, sending):
        size, last, devices, at, many = (
            (Y, Y // 2, ydev, cy, X) if part_at == 0 else (X, X // 2, xdev, cx, Y)
        )
        away = hop - 1 if sending else hop
        owner = (at - away + size) % size if way == 0 else (at + away) % size
        group = piece(way, hop, last, many)
        rows = pl.ds(part_at * half, half)
        ref = gat.at[group, owner, rows] if part_at == 0 else gat.at[owner, group, rows]
        return copy(ref, ref, ga_ss.at[0], g2_rs.at[hop - 1], devices[way])

    def gather_send(hop):
        if hop <= X // 2:
            for part_at in range(2):
                for way in range(2):
                    g2_copy(part_at, way, hop, True).start()

    def gather_wait(hop):
        if hop <= X // 2:
            arrived(g2_rs.at[hop - 1], gat.at[pl.ds(0, 2 if hop < X // 2 else 1)])

    def sb_copy(zz, sending):
        target = zz * 2 + (1 - r if sending else r)
        return copy(part.at[target], sib.at[zz], sb_ss.at[0], sb_rs.at[zz], sibling)

    def project(lo, hi):
        for o in range(lo, hi):
            hop = H - (o + 1) // 2
            zz = (z + Z + hop * (2 * (o % 2) - 1)) % Z
            gated = gat[cx, cy]
            for core in range(2):
                target = zz * 2 + ((1 - r) if core == 0 else r)
                part[target] = jnp.dot(
                    gated, wv[target], preferred_element_type=F32
                ).astype(BF16)
                if core == 0:
                    sb_copy(zz, True).start()

    halves_of = (pl.ds(0, half), pl.ds(half, half))

    def rr_copy(way, step, k):
        return copy(
            rs_out.at[way, step, halves_of[k]], rs_in.at[way, step, halves_of[k]],
            rr_ss.at[0], rr_rs.at[way, step, k], zdev[way],
        )

    def pair_sum(zz, k):
        return part[zz * 2 + r, halves_of[k]].astype(F32) + sib[zz, halves_of[k]].astype(F32)

    def reduce_target(way, step):
        away = H - step
        return (z + away) % Z if way == 0 else (z - away + Z) % Z

    def reduce_piece(way, step, k, arrived):
        total = pair_sum(reduce_target(way, step), k)
        if arrived:
            rr_copy(way, step - 1, k).wait_recv()
            total = total + rs_in[way, step - 1, halves_of[k]].astype(F32)
        rs_out[way, step, halves_of[k]] = total.astype(BF16)
        rr_copy(way, step, k).start()

    def reduce_first():
        sb_copy((z + H) % Z, False).wait_recv()
        for way in range(2):
            reduce_piece(way, 0, way, False)
        if H > 1:
            for way in range(2):
                sb_copy(reduce_target(way, 1), False).wait_recv()
                reduce_piece(way, 1, 1 - way, False)

    def reduce_second():
        if H > 1:
            for way in range(2):
                reduce_piece(way, 1, way, True)

    def reduce_step(step, k):
        if step < H:
            for way in range(2):
                if k == 0:
                    sb_copy(reduce_target(way, step), False).wait_recv()
                reduce_piece(way, step, k, True)

    def reduce_last():
        sb_copy(z, False).wait_recv()
        for k in range(2):
            total = pair_sum(z, k)
            for way in range(2):
                if H > 1 or way == k:
                    rr_copy(way, H - 1, k).wait_recv()
                    total = total + rs_in[way, H - 1, halves_of[k]].astype(F32)
            mixed_ref[halves_of[k]] = total.astype(BF16)

    active = c % 2 == r

    def fw_copy(own, n):
        ref = cot_t.at[pl.ds(n * Y, Y), own_rows if own else other_rows]
        return copy(ref, ref, fw_ss.at[0], fw_rs.at[0 if own else 1], sibling)

    def ex_copy(way, n, sending):
        side = odd if sending else 1 - odd
        low = pl.multiple_of(side * (R // 2) + way * (R // 4), R // 4)
        ref = cot_t.at[pl.ds(n * Y, Y), pl.ds(low, R // 4)]
        return copy(ref, ref, ex_ss.at[0], ex_rs.at[way, n], zdev[way])

    def group_arrived(n):
        def some(count):
            return lambda: arrived(aa_rs.at[n], cot_t.at[pl.ds(0, count), pl.ds(0, R // 2)])

        pl.when(n == cx)(some(Y - 1))
        pl.when(n != cx)(some(Y))

    def pass_group(n):
        group_arrived(n)
        for way in range(2):
            ex_copy(way, n, True).start()

    reach = (z - c // 2 + Z) % Z

    def pass_on(*distances):
        chosen = [reach == away % Z for away in set(distances) | {-away for away in distances}]

        @pl.when(jnp.logical_and(active, functools.reduce(jnp.logical_or, chosen)))
        def _():
            cot_t[c, own_rows] = cot_all[c, own_rows]
            pl.loop(0, X)(pass_group)

    def hand_own():
        @pl.when(active)
        def _():
            for n in range(X):
                fw_copy(True, n).start()

    def hand_group(n):
        for way in range(2):
            ex_copy(way, n, False).wait_recv()
        fw_copy(False, n).start()

    def hand_over():
        pl.when(active)(lambda: pl.loop(0, X)(hand_group))

    def handed(own):
        rows = pl.ds(0, R // 2)
        pl.when(jnp.logical_not(active))(lambda: arrived(fw_rs.at[0 if own else 1], cot_t.at[:, rows]))

    def drain_passed():
        @pl.when(active)
        def _():
            left(ex_ss.at[0], cot_t.at[:, pl.ds(0, R // 2)])
            left(fw_ss.at[0], cot_t)
            left(aa_ss.at[0], cot_t.at[pl.ds(0, Z - 1), pl.ds(0, R // 2)])

        @pl.when(jnp.logical_not(active))
        def _():
            left(aa_ss.at[0], cot_t.at[pl.ds(0, Z), pl.ds(0, R // 2)])

    def wait_weights():
        pltpu.make_async_copy(wv, wv, w_sem.at[0]).wait()

    def begin():
        for n in (0, 1, 2):
            load(n).wait()
        src[...] = k_ref[...].astype(F32) * v_ref[...].astype(F32)
        spread_rates()
        local_states(src, True)

    def first_sends():
        load(3).wait()
        send_states(0)
        ag_start()
        spread(0)

    def filter_spectrum_loaded():
        for n in (5, 6, 7):
            load(n).wait()
        filter_spectrum()

    def gate():
        carry_in(True)
        add_carry(True, conv)
        gat[cx, cy] = (q_ref[...].astype(F32) * conv[...]).astype(BF16)
        gather_first()

    def multiply_back(distances, cores, first=False):
        if not distances:
            return
        zs = [(z + Z + away) % Z for away in distances]
        blocks = [zz * 2 + core for zz in zs for core in cores]
        total = lax.dot_general(
            jnp.concatenate([cot_all[n] for n in blocks], axis=1),
            jnp.concatenate([wv[n] for n in blocks], axis=1),
            (((1,), (1,)), ((), ())), preferred_element_type=F32,
        )
        back[...] = total if first else back[...] + total

    def back_states():
        qg_ref[...] = (back[...] * conv[...]).astype(BF16)
        cgr[...] = back[...] * q_ref[...].astype(F32)
        local_states(cgr, False)
        send_states(1)

    def key_value():
        carry_in(False)
        add_carry(False, mix)
        kg_ref[...] = (mix[...] * v_ref[...].astype(F32)).astype(BF16)
        vg_ref[...] = (mix[...] * k_ref[...].astype(F32)).astype(BF16)

    def mixed_done():
        reduce_last()

    def weight_product(rows, first):
        total = lax.dot_general(
            gat[:, :, rows].reshape(N * half, C), cot_t[:, rows].reshape(N * half, C),
            (((0,), (0,)), ((), ())), preferred_element_type=F32,
        )
        if first:
            wacc[...] = total
        else:
            wg_ref[...] = (wacc[...] + total).astype(BF16)

    def drain():
        drain_states(0)
        drain_states(1)
        left(ag_ss.at[0], cot_all.at[pl.ds(0, Z - 1)])
        left(cs_ss.at[0], cot_all.at[pl.ds(0, Z)])
        left(sb_ss.at[0], sib)
        left(rr_ss.at[0], cot_all.at[pl.ds(0, Z - 1)])
        left(ga_ss.at[0], cot_all.at[pl.ds(0, N - 1)])
        drain_passed()

    def arrive(hop, k):
        if hop < H:
            ag_arrive(hop, k)

    assert H <= 4 and X == Y and N == 2 * Z
    def scatter_at(away):
        if away <= H:
            scatter(away, away + 1)
            if away < H:
                scatter(-away, -away + 1)

    def projects(lo, hi):
        return lambda: project(min(lo, Z), min(hi, Z))

    same, both = (r,), (0, 1)
    steps = [
        ("begin", begin),
        ("barrier", lambda: pl.semaphore_wait(barrier, N - 1 + 3)),
        ("first_sends", first_sends),
        ("weights", spread_weights),
        ("taps", filter_taps),
        ("spectrum", filter_spectrum_loaded),
        ("send_rows", lambda: send_rows(0)),
        ("arrive1a", lambda: arrive(1, 0)),
        ("convolve", lambda: convolve(src, True, conv)),
        ("arrive1b", lambda: arrive(1, 1)),
        ("wait_rows", lambda: wait_rows(0)),
        ("gate", gate),
        ("scatter01", lambda: scatter(-min(1, H - 1), min(1, H - 1) + 1)),
        ("arrive2a", lambda: arrive(2, 0)),
        ("wait_weights", wait_weights),
        ("project_1", projects(0, 3)),
        ("arrive2b", lambda: arrive(2, 1)),
        ("scatter2", lambda: scatter_at(2) if H > 2 else None),
        ("project_2", projects(3, 5)),
        ("arrive3a", lambda: arrive(3, 0)),
        ("project_3", projects(5, Z)),
        ("arrive3b", lambda: arrive(3, 1)),
        ("reduce_first", reduce_first),
        ("scatter3", lambda: scatter_at(3) if H > 3 else None),
        ("sibling_near", lambda: sibling_here(0)),
        ("back_near", lambda: multiply_back(near, both, True)),
        ("gather1", gather_first_here),
        ("gather2_send1", lambda: gather_send(1)),
        ("arrive_last", lambda: (ag_arrive(H, 0), ag_arrive(H, 1))),
        ("scatter_last", lambda: scatter_at(H)),
        ("back_far_same", lambda: multiply_back(far, same)),
        ("reduce_second", reduce_second),
        ("pass_01", lambda: pass_on(*range(min(2, H)))),
        ("sibling_far", lambda: sibling_here(1)),
        ("back_far_other", lambda: multiply_back(far, (1 - r,))),
        ("back_states", back_states),
        ("pass_2", lambda: pass_on(2) if H > 2 else None),
        ("pass_3", lambda: pass_on(3) if H > 3 else None),
        ("reduce2a", lambda: reduce_step(2, 0)),
        ("correlate", lambda: convolve(cgr, False, mix)),
        ("reduce2b", lambda: reduce_step(2, 1)),
        ("pass_last", lambda: pass_on(H)),
        ("gather2_wait1", lambda: gather_wait(1)),
        ("gather2_send2", lambda: gather_send(2)),
        ("send_back_rows", lambda: send_rows(1)),
        ("hand_own", hand_own),
        ("reduce3a", lambda: reduce_step(3, 0)),
        ("reduce3b", lambda: reduce_step(3, 1)),
        ("hand_over", hand_over),
        ("wait_back_rows", lambda: wait_rows(1)),
        ("key_value", key_value),
        ("handed_own", lambda: handed(True)),
        ("gather2_wait2", lambda: gather_wait(2)),
        ("weight_own", lambda: weight_product(own_rows, True)),
        ("mixed_done", mixed_done),
        ("handed_over", lambda: handed(False)),
        ("weight_other", lambda: weight_product(other_rows, False)),
        ("drain", drain),
    ]
    for name, step in steps:
        step()


def transforms(R):
    angle = np.pi / (2 * R) * (np.outer(2 * np.arange(R) + 1, np.arange(R)) % (4 * R))
    there = np.concatenate([np.cos(angle), -np.sin(angle)])
    result = []
    for table in (there, there.T / R):
        high = table.astype(np.float32).astype(ml_dtypes.bfloat16)
        low = (table - high.astype(np.float64)).astype(ml_dtypes.bfloat16)
        result.append(jnp.asarray(np.concatenate([high, low, high], axis=1)))
    return result


def finish(*refs):
    count = len(refs) // 2
    given, made, sem = refs[:count], refs[count : 2 * count], refs[-1]
    copies = [pltpu.make_async_copy(a, b, sem.at[n]) for n, (a, b) in enumerate(zip(given, made))]
    for one in copies:
        one.start()
    for one in copies:
        one.wait()


def solution(mesh):
    N = mesh.shape["context"]
    X = math.isqrt(N)
    Y = N // X
    Z = mesh.shape["tensor"] // 2
    H = Z // 2

    def shards(query_rows, key_rows, value_rows, residue, decay_rate, out_weight, cotangent):
        R, C = query_rows.shape
        M = residue.shape[0]
        small = jax.ShapeDtypeStruct((R, C), BF16)
        dma = pltpu.SemaphoreType.DMA
        top = max(X // 2, Y // 2)
        anywhere = pl.BlockSpec(memory_space=pl.ANY)
        results = (small, small, small, small, jax.ShapeDtypeStruct((C, C), BF16))
        made = pl.pallas_call(
            functools.partial(body, X, Y, Z),
            out_shape=tuple(pltpu.VMEM(one.shape, BF16) for one in results),
            in_specs=[anywhere] * 9,
            out_specs=(pl.BlockSpec(memory_space=pltpu.VMEM),) * 5,
            scratch_shapes=[
                pltpu.VMEM((2 * Z, C, C), BF16),
                pltpu.VMEM((2 * Z, R, C), BF16),
                pltpu.VMEM((N, R, C), BF16),
                pltpu.VMEM((X, Y, R, C), BF16),
                pltpu.VMEM((2 * Z, R, C), BF16),
                pltpu.VMEM((Z, R, C), BF16),
                pltpu.VMEM((2, H, R, C), BF16),
                pltpu.VMEM((2, H, R, C), BF16),
                pltpu.VMEM((2, Y, M, C), F32),
                pltpu.VMEM((2, X, M, C), F32),
                pltpu.VMEM((R, C), BF16),
                pltpu.VMEM((R, C), BF16),
                pltpu.VMEM((R, C), BF16),
                pltpu.VMEM((M, C), F32),
                pltpu.VMEM((M, C), F32),
                pltpu.VMEM((2 * R, 3 * R), BF16),
                pltpu.VMEM((R, 6 * R), BF16),
                dma((8,)),
                pltpu.VMEM((R, C), F32),
                pltpu.VMEM((R, C), F32),
                pltpu.VMEM((R, C), F32),
                pltpu.VMEM((R, C), F32),
                pltpu.VMEM((R, C), F32),
                pltpu.VMEM((R, C), F32),
                pltpu.VMEM((2 * R, C), F32),
                pltpu.VMEM((C, C), F32),
                pltpu.VMEM((M, 8, C), F32),
                pltpu.VMEM((M, 8, C), F32),
                pltpu.VMEM((M, 8, C), F32),
                pltpu.VMEM((M, 8, C), F32),
                dma((1,)),
                dma((1,)),
                dma((2, H, 2)),
                dma((1,)),
                dma((2,)),
                dma((1,)),
                dma((X,)),
                dma((1,)),
                dma((2,)),
                dma((1,)),
                dma((2, X)),
                dma((2,)),
                dma((2,)),
                dma((2,)),
                dma((2,)),
                dma((1,)),
                dma((1,)),
                dma((top,)),
                dma((1,)),
                dma((Z,)),
                dma((1,)),
                dma((2, H, 2)),
            ],
            compiler_params=pltpu.CompilerParams(
                collective_id=0, has_side_effects=True, vmem_limit_bytes=56 * 1024 * 1024
            ),
            name="hyena_block",
        )(query_rows, key_rows, value_rows, residue, decay_rate, out_weight, cotangent, *transforms(R))
        return pl.pallas_call(
            finish,
            out_shape=results,
            in_specs=[anywhere] * 5,
            out_specs=(anywhere,) * 5,
            scratch_shapes=[dma((5,))],
            compiler_params=pltpu.CompilerParams(vmem_limit_bytes=1024 * 1024),
            name="hand_out",
        )(*made)

    placed = (
        P("context", "tensor"),
        P("context", "tensor"),
        P("context", "tensor"),
        P(None, "tensor"),
        P(None, "tensor"),
        P("tensor", None),
        P("context", "tensor"),
    )
    return jax.shard_map(
        shards,
        mesh=mesh,
        in_specs=placed,
        out_specs=(
            P("context", "tensor"),
            P("context", "tensor"),
            P("context", "tensor"),
            P("context", "tensor"),
            P("tensor", "context"),
        ),
        check_vma=False,
    )
```

```python
import functools
import math

import jax
import jax.numpy as jnp
import ml_dtypes
import numpy as np
from jax import lax
from jax.experimental import pallas as pl
from jax.experimental.pallas import tpu as pltpu
from jax.sharding import PartitionSpec as P

MESH = pl.DeviceIdType.MESH
F32 = jnp.float32
BF16 = jnp.bfloat16
LANES = 128


def body(
    X, Y, Z,
    q_in, k_in, v_in, res_in, dec_in, w_ref, cot_in, fold_in, unfold_in,
    mixed_ref, qg_ref, kg_ref, vg_ref, wg_ref,
    wv, cot_all, cot_t, gat, part, sib, rs_out, rs_in, states, row_states,
    q_ref, k_ref, v_ref, res_ref, dec_ref, fold, unfold, in_sem,
    src, cgr, conv, back, mix, taps, taps_hat, wacc, rates, weights, powers, starts,
    w_sem, ag_ss, ag_rs, cs_ss, cs_rs, aa_ss, aa_rs, fw_ss, fw_rs, ex_ss, ex_rs, st_ss, st_rs, ro_ss, ro_rs,
    ga_ss, g1_rs, g2_rs, sb_ss, sb_rs, rr_ss, rr_rs,
):
    N = X * Y
    R, C = q_in.shape
    M = dec_in.shape[0]
    T = R // 8
    G = C // LANES
    H = Z // 2
    c = lax.axis_index("context")
    j = lax.axis_index("tensor")
    z, r = j // 2, j % 2
    cx, cy = c // Y, c % Y
    other = z * 2 + 1 - r
    mine = (c, j)
    sibling = (c, other)
    zdev = [(c, ((z + 1) % Z) * 2 + r), (c, ((z + Z - 1) % Z) * 2 + r)]
    xdev = [(((cx + 1) % X) * Y + cy, j), (((cx + X - 1) % X) * Y + cy, j)]
    ydev = [(cx * Y + (cy + 1) % Y, j), (cx * Y + (cy + Y - 1) % Y, j)]

    def copy(source, target, send_sem, recv_sem, device):
        return pltpu.make_async_remote_copy(
            src_ref=source, dst_ref=target, send_sem=send_sem, recv_sem=recv_sem,
            device_id=device, device_id_type=MESH,
        )

    def arrived(sem, ref):
        copy(ref, ref, sem, sem, mine).wait_recv()

    def left(sem, ref):
        copy(ref, ref, sem, sem, mine).wait_send()

    def lanes_of(g):
        return pl.ds(pl.multiple_of(g * LANES, LANES), LANES)

    barrier = pltpu.get_barrier_semaphore()
    for device in zdev + [sibling]:
        pl.semaphore_signal(barrier, inc=1, device_id=device, device_id_type=MESH)

    @pl.loop(0, N)
    def _(p):
        @pl.when(p != c)
        def _():
            pl.semaphore_signal(barrier, inc=1, device_id=(p, j), device_id_type=MESH)

    loads = (
        (k_in, k_ref), (v_in, v_ref), (dec_in, dec_ref), (cot_in, cot_all.at[j]), (res_in, res_ref),
        (fold_in, fold), (q_in, q_ref), (unfold_in, unfold),
    )

    def load(n):
        return pltpu.make_async_copy(*loads[n], in_sem.at[n])

    for n in range(len(loads)):
        load(n).start()

    def w_copy(n):
        return pltpu.make_async_copy(
            w_ref.at[:, pl.ds(pl.multiple_of(n * C, LANES), C)], wv.at[n], w_sem.at[0]
        )

    @pl.loop(0, 2 * Z)
    def _(n):
        w_copy(n).start()

    rows8 = lax.broadcasted_iota(jnp.int32, (8, LANES), 0).astype(F32)

    def spread_weights():
        load(4).wait()
        weight = res_ref[...] * jnp.sqrt(dec_ref[...])
        for m in range(M):
            weights[m] = jnp.broadcast_to(weight[m : m + 1], (8, C))

    def spread_rates():
        for m in range(M):
            rate = jnp.broadcast_to(dec_ref[pl.ds(m, 1), :], (8, C))
            rates[m] = rate
            powers[m] = jnp.exp(-8.0 * rate)

    def local_states(values, forward):
        way = 0 if forward else 1

        @pl.loop(0, G)
        def _(g):
            lanes = lanes_of(g)
            tiles = [values[pl.ds(8 * a, 8), lanes] for a in range(T)]
            if not forward:
                tiles = tiles[::-1]

            @pl.loop(0, M // 8)
            def _(eight):
                sums = []
                for inner in range(8):
                    m = eight * 8 + inner
                    step = powers[m, :, lanes]
                    total = tiles[0]
                    for tile in tiles[1:]:
                        total = total * step + tile
                    reach = 7.0 - rows8 if forward else rows8
                    total = total * jnp.exp(-rates[m, :, lanes] * reach)
                    sums.append(jnp.sum(total, axis=0, keepdims=True))
                modes = pl.ds(pl.multiple_of(eight * 8, 8), 8)
                states[way, cy, modes, lanes] = jnp.concatenate(sums, axis=0)

    def filter_taps():
        @pl.loop(0, G)
        def _(g):
            lanes = lanes_of(g)

            def add_mode(m, tiles):
                step = powers[m, :, lanes]
                term = weights[m, :, lanes] * jnp.exp(-rates[m, :, lanes] * rows8)
                new = []
                for a in range(T):
                    new.append(tiles[a] + term)
                    term = term * step
                return tuple(new)

            zero = jnp.zeros((8, LANES), F32)
            tiles = lax.fori_loop(0, M, add_mode, (zero,) * T, unroll=4)
            for a in range(T):
                taps[pl.ds(8 * a, 8), lanes] = tiles[a]

    width = min(C, 256)

    def halves(value):
        high = value.astype(BF16)
        return high, (value - high.astype(F32)).astype(BF16)

    def analyse(value):
        high, low = halves(value)
        return jnp.dot(fold[...], jnp.concatenate([high, high, low]), preferred_element_type=F32)

    def filter_spectrum():
        for lo in range(0, C, width):
            lanes = slice(lo, lo + width)
            taps_hat[:, lanes] = analyse(taps[:, lanes])

    def convolve(values, forward, out):
        for lo in range(0, C, width):
            lanes = slice(lo, lo + width)
            both = analyse(values[:, lanes])
            real, imag = both[:R], both[R:]
            tap_real, tap_imag = taps_hat[:R, lanes], taps_hat[R:, lanes]
            if forward:
                new_real = tap_real * real - tap_imag * imag
                new_imag = tap_real * imag + tap_imag * real
            else:
                new_real = tap_real * real + tap_imag * imag
                new_imag = tap_real * imag - tap_imag * real
            real_high, real_low = halves(new_real)
            imag_high, imag_low = halves(new_imag)
            out[:, lanes] = jnp.dot(
                unfold[...],
                jnp.concatenate([real_high, imag_high, real_high, imag_high, real_low, imag_low]),
                preferred_element_type=F32,
            )

    def carry_in(forward):
        way = 0 if forward else 1
        decay = jnp.exp(-float(R) * dec_ref[...])
        row_decay = jnp.exp(-float(R * Y) * dec_ref[...])

        def add_row(n, total):
            return total * row_decay + row_states[way, n if forward else X - 1 - n]

        def add_block(n, total):
            return total * decay + states[way, n if forward else Y - 1 - n]

        total = lax.fori_loop(0, cx if forward else X - 1 - cx, add_row, jnp.zeros((M, C), F32))
        total = lax.fori_loop(0, cy if forward else Y - 1 - cy, add_block, total)
        for m in range(M):
            starts[m] = weights[m] * total[m : m + 1]

    def add_carry(forward, out):
        @pl.loop(0, G)
        def _(g):
            lanes = lanes_of(g)

            def add_mode(m, tiles):
                rate, step = rates[m, :, lanes], powers[m, :, lanes]
                term = starts[m, :, lanes] * jnp.exp(-rate * ((rows8 + 1.0) if forward else (8.0 - rows8)))
                new = []
                for a in range(T):
                    new.append(tiles[a] + term)
                    term = term * step
                return tuple(new)

            order = list(range(T)) if forward else list(range(T))[::-1]
            tiles = lax.fori_loop(
                0, M, add_mode, tuple(out[pl.ds(8 * a, 8), lanes] for a in order), unroll=4
            )
            for n, a in enumerate(order):
                out[pl.ds(8 * a, 8), lanes] = tiles[n]

    def state_copy(way, y, sending):
        ref = states.at[way, cy if sending else y]
        sem = st_rs.at[way]
        return copy(ref, ref, st_ss.at[way], sem, (cx * Y + y, j))

    def row_copy(way, x, sending):
        ref = row_states.at[way, cx if sending else x]
        sem = ro_rs.at[way]
        return copy(ref, ref, ro_ss.at[way], sem, (x * Y + cy, j))

    def others(count, here, act):
        @pl.loop(0, count)
        def _(n):
            pl.when(n != here)(lambda: act(n))

    def send_states(way):
        others(Y, cy, lambda y: state_copy(way, y, True).start())

    def send_rows(way):
        arrived(st_rs.at[way], states.at[way, pl.ds(0, Y - 1)])
        decay = jnp.exp(-float(R) * dec_ref[...])
        order = range(Y) if way == 0 else range(Y)[::-1]
        total = states[way, order[0]]
        for y in order[1:]:
            total = total * decay + states[way, y]
        row_states[way, cx] = total

        others(X, cx, lambda x: row_copy(way, x, True).start())

    def wait_rows(way):
        arrived(ro_rs.at[way], row_states.at[way, pl.ds(0, X - 1)])

    def drain_states(way):
        left(st_ss.at[way], states.at[way, pl.ds(0, Y - 1)])
        left(ro_ss.at[way], row_states.at[way, pl.ds(0, X - 1)])

    near = list(range(-min(2, H - 1), min(2, H - 1) + 1))
    far = [away for away in range(-H + 1, H + 1) if away not in near]

    def piece(way, hop, last, size):
        if hop < last:
            return pl.ds(0, size)
        return pl.ds(way * (size // 2), size // 2)

    def ag_copy(way, hop, k, sending):
        away = hop - 1 if sending else hop
        owner = (z - away + Z) % Z if way == 0 else (z + away) % Z
        ref = cot_all.at[owner * 2 + r, pl.ds(k * (R // 2), R // 2)]
        return copy(ref, ref, ag_ss.at[0], ag_rs.at[way, hop - 1, k], zdev[way])

    def ag_pieces(hop):
        return [(way, k) for k in range(2) for way in range(2) if hop < H or way == k]

    def spread(away):
        ref = cot_all.at[(z + Z + away) % Z * 2 + r]
        group = 0 if away in near else 1
        copy(ref, ref, cs_ss.at[0], cs_rs.at[group], sibling).start()

    def sibling_here(group):
        arrived(cs_rs.at[group], cot_all.at[pl.ds(0, len((near, far)[group]))])

    odd = z % 2
    own_rows = pl.ds(pl.multiple_of(odd * (R // 2), R // 2), R // 2)
    other_rows = pl.ds(pl.multiple_of((1 - odd) * (R // 2), R // 2), R // 2)

    def aa_copy(zz):
        owner = zz * 2 + r
        return copy(
            cot_all.at[owner, own_rows], cot_t.at[c, own_rows], aa_ss.at[0], aa_rs.at[cx], (owner, j)
        )

    def scatter(lo, hi):
        count = hi - lo

        @pl.loop(0, count)
        def _(n):
            zz = (z + Z + lo + (c // 2 + n) % count) % Z

            @pl.when(zz * 2 + r != c)
            def _():
                aa_copy(zz).start()

    def ag_start():
        for way, k in ag_pieces(1):
            ag_copy(way, 1, k, True).start()

    def ag_arrive(hop, half_at):
        for way, k in ag_pieces(hop):
            if k == half_at:
                ag_copy(way, hop, k, False).wait_recv()
                if (way, k) in ag_pieces(hop + 1) and hop < H:
                    ag_copy(way, hop + 1, k, True).start()
        if half_at == 1:
            spread(hop)
            if hop < H:
                spread(-hop)

    half = R // 2

    def gather_first():
        for part_at in range(2):
            ref = gat.at[cx, cy, pl.ds(part_at * half, half)]
            for away in range(1, X):
                to = ((cx + away) % X) * Y + cy if part_at == 0 else cx * Y + (cy + away) % Y
                copy(ref, ref, ga_ss.at[0], g1_rs.at[0], (to, j)).start()

    def gather_first_here():
        arrived(g1_rs.at[0], gat.at[0, pl.ds(0, X - 1)])

    def g2_copy(part_at, way, hop, sending):
        size, last, devices, at, many = (
            (Y, Y // 2, ydev, cy, X) if part_at == 0 else (X, X // 2, xdev, cx, Y)
        )
        away = hop - 1 if sending else hop
        owner = (at - away + size) % size if way == 0 else (at + away) % size
        group = piece(way, hop, last, many)
        rows = pl.ds(part_at * half, half)
        ref = gat.at[group, owner, rows] if part_at == 0 else gat.at[owner, group, rows]
        return copy(ref, ref, ga_ss.at[0], g2_rs.at[hop - 1], devices[way])

    def gather_send(hop):
        if hop <= X // 2:
            for part_at in range(2):
                for way in range(2):
                    g2_copy(part_at, way, hop, True).start()

    def gather_wait(hop):
        if hop <= X // 2:
            arrived(g2_rs.at[hop - 1], gat.at[pl.ds(0, 2 if hop < X // 2 else 1)])

    def sb_copy(zz, sending):
        target = zz * 2 + (1 - r if sending else r)
        return copy(part.at[target], sib.at[zz], sb_ss.at[0], sb_rs.at[zz], sibling)

    def project(lo, hi):
        for o in range(lo, hi):
            hop = H - (o + 1) // 2
            zz = (z + Z + hop * (2 * (o % 2) - 1)) % Z
            gated = gat[cx, cy]
            for core in range(2):
                target = zz * 2 + ((1 - r) if core == 0 else r)
                part[target] = jnp.dot(
                    gated, wv[target], preferred_element_type=F32
                ).astype(BF16)
                if core == 0:
                    sb_copy(zz, True).start()

    halves_of = (pl.ds(0, half), pl.ds(half, half))

    def rr_copy(way, step, k):
        return copy(
            rs_out.at[way, step, halves_of[k]], rs_in.at[way, step, halves_of[k]],
            rr_ss.at[0], rr_rs.at[way, step, k], zdev[way],
        )

    def pair_sum(zz, k):
        return part[zz * 2 + r, halves_of[k]].astype(F32) + sib[zz, halves_of[k]].astype(F32)

    def reduce_target(way, step):
        away = H - step
        return (z + away) % Z if way == 0 else (z - away + Z) % Z

    def reduce_piece(way, step, k, arrived):
        total = pair_sum(reduce_target(way, step), k)
        if arrived:
            rr_copy(way, step - 1, k).wait_recv()
            total = total + rs_in[way, step - 1, halves_of[k]].astype(F32)
        rs_out[way, step, halves_of[k]] = total.astype(BF16)
        rr_copy(way, step, k).start()

    def reduce_first():
        sb_copy((z + H) % Z, False).wait_recv()
        for way in range(2):
            reduce_piece(way, 0, way, False)
        if H > 1:
            for way in range(2):
                sb_copy(reduce_target(way, 1), False).wait_recv()
                reduce_piece(way, 1, 1 - way, False)

    def reduce_second():
        if H > 1:
            for way in range(2):
                reduce_piece(way, 1, way, True)

    def reduce_step(step, k):
        if step < H:
            for way in range(2):
                if k == 0:
                    sb_copy(reduce_target(way, step), False).wait_recv()
                reduce_piece(way, step, k, True)

    def reduce_last():
        sb_copy(z, False).wait_recv()
        for k in range(2):
            total = pair_sum(z, k)
            for way in range(2):
                if H > 1 or way == k:
                    rr_copy(way, H - 1, k).wait_recv()
                    total = total + rs_in[way, H - 1, halves_of[k]].astype(F32)
            mixed_ref[halves_of[k]] = total.astype(BF16)

    active = c % 2 == r

    def fw_copy(own, n):
        ref = cot_t.at[pl.ds(n * Y, Y), own_rows if own else other_rows]
        return copy(ref, ref, fw_ss.at[0], fw_rs.at[0 if own else 1], sibling)

    def ex_copy(way, n, sending):
        side = odd if sending else 1 - odd
        low = pl.multiple_of(side * (R // 2) + way * (R // 4), R // 4)
        ref = cot_t.at[pl.ds(n * Y, Y), pl.ds(low, R // 4)]
        return copy(ref, ref, ex_ss.at[0], ex_rs.at[way, n], zdev[way])

    def group_arrived(n):
        def some(count):
            return lambda: arrived(aa_rs.at[n], cot_t.at[pl.ds(0, count), pl.ds(0, R // 2)])

        pl.when(n == cx)(some(Y - 1))
        pl.when(n != cx)(some(Y))

    def pass_group(n):
        group_arrived(n)
        for way in range(2):
            ex_copy(way, n, True).start()

    reach = (z - c // 2 + Z) % Z

    def pass_on(*distances):
        chosen = [reach == away % Z for away in set(distances) | {-away for away in distances}]

        @pl.when(jnp.logical_and(active, functools.reduce(jnp.logical_or, chosen)))
        def _():
            cot_t[c, own_rows] = cot_all[c, own_rows]
            pl.loop(0, X)(pass_group)

    def hand_own():
        @pl.when(active)
        def _():
            for n in range(X):
                fw_copy(True, n).start()

    def hand_group(n):
        for way in range(2):
            ex_copy(way, n, False).wait_recv()
        fw_copy(False, n).start()

    def hand_over():
        pl.when(active)(lambda: pl.loop(0, X)(hand_group))

    def handed(own):
        rows = pl.ds(0, R // 2)
        pl.when(jnp.logical_not(active))(lambda: arrived(fw_rs.at[0 if own else 1], cot_t.at[:, rows]))

    def drain_passed():
        @pl.when(active)
        def _():
            left(ex_ss.at[0], cot_t.at[:, pl.ds(0, R // 2)])
            left(fw_ss.at[0], cot_t)
            left(aa_ss.at[0], cot_t.at[pl.ds(0, Z - 1), pl.ds(0, R // 2)])

        @pl.when(jnp.logical_not(active))
        def _():
            left(aa_ss.at[0], cot_t.at[pl.ds(0, Z), pl.ds(0, R // 2)])

    def wait_weights():
        pltpu.make_async_copy(wv, wv, w_sem.at[0]).wait()

    def begin():
        for n in (0, 1, 2):
            load(n).wait()
        src[...] = k_ref[...].astype(F32) * v_ref[...].astype(F32)
        spread_rates()
        local_states(src, True)

    def first_sends():
        load(3).wait()
        send_states(0)
        ag_start()
        spread(0)

    def filter_spectrum_loaded():
        for n in (5, 6, 7):
            load(n).wait()
        filter_spectrum()

    def gate():
        carry_in(True)
        add_carry(True, conv)
        gat[cx, cy] = (q_ref[...].astype(F32) * conv[...]).astype(BF16)
        gather_first()

    def multiply_back(distances, cores, first=False):
        if not distances:
            return
        zs = [(z + Z + away) % Z for away in distances]
        blocks = [zz * 2 + core for zz in zs for core in cores]
        total = lax.dot_general(
            jnp.concatenate([cot_all[n] for n in blocks], axis=1),
            jnp.concatenate([wv[n] for n in blocks], axis=1),
            (((1,), (1,)), ((), ())), preferred_element_type=F32,
        )
        back[...] = total if first else back[...] + total

    def back_states():
        qg_ref[...] = (back[...] * conv[...]).astype(BF16)
        cgr[...] = back[...] * q_ref[...].astype(F32)
        local_states(cgr, False)
        send_states(1)

    def key_value():
        carry_in(False)
        add_carry(False, mix)
        kg_ref[...] = (mix[...] * v_ref[...].astype(F32)).astype(BF16)
        vg_ref[...] = (mix[...] * k_ref[...].astype(F32)).astype(BF16)

    def mixed_done():
        reduce_last()

    def weight_product(rows, first):
        total = lax.dot_general(
            gat[:, :, rows].reshape(N * half, C), cot_t[:, rows].reshape(N * half, C),
            (((0,), (0,)), ((), ())), preferred_element_type=F32,
        )
        if first:
            wacc[...] = total
        else:
            wg_ref[...] = (wacc[...] + total).astype(BF16)

    def drain():
        drain_states(0)
        drain_states(1)
        left(ag_ss.at[0], cot_all.at[pl.ds(0, Z - 1)])
        left(cs_ss.at[0], cot_all.at[pl.ds(0, Z)])
        left(sb_ss.at[0], sib)
        left(rr_ss.at[0], cot_all.at[pl.ds(0, Z - 1)])
        left(ga_ss.at[0], cot_all.at[pl.ds(0, N - 1)])
        drain_passed()

    def arrive(hop, k):
        if hop < H:
            ag_arrive(hop, k)

    assert H <= 4 and X == Y and N == 2 * Z
    def scatter_at(away):
        if away <= H:
            scatter(away, away + 1)
            if away < H:
                scatter(-away, -away + 1)

    def projects(lo, hi):
        return lambda: project(min(lo, Z), min(hi, Z))

    same, both = (r,), (0, 1)
    steps = [
        ("begin", begin),
        ("barrier", lambda: pl.semaphore_wait(barrier, N - 1 + 3)),
        ("first_sends", first_sends),
        ("weights", spread_weights),
        ("taps", filter_taps),
        ("spectrum", filter_spectrum_loaded),
        ("send_rows", lambda: send_rows(0)),
        ("arrive1a", lambda: arrive(1, 0)),
        ("convolve", lambda: convolve(src, True, conv)),
        ("arrive1b", lambda: arrive(1, 1)),
        ("wait_rows", lambda: wait_rows(0)),
        ("gate", gate),
        ("arrive2a", lambda: arrive(2, 0)),
        ("wait_weights", wait_weights),
        ("project_1", projects(0, 3)),
        ("arrive2b", lambda: arrive(2, 1)),
        ("scatter_near", lambda: scatter(near[0], near[-1] + 1)),
        ("project_2", projects(3, 5)),
        ("arrive3a", lambda: arrive(3, 0)),
        ("project_3", projects(5, Z)),
        ("arrive3b", lambda: arrive(3, 1)),
        ("reduce_first", reduce_first),
        ("scatter3", lambda: scatter_at(3) if H > 3 else None),
        ("sibling_near", lambda: sibling_here(0)),
        ("back_near", lambda: multiply_back(near, both, True)),
        ("arrive_last", lambda: (ag_arrive(H, 0), ag_arrive(H, 1))),
        ("scatter_last", lambda: scatter_at(H)),
        ("gather1", gather_first_here),
        ("gather2_send1", lambda: gather_send(1)),
        ("back_far_same", lambda: multiply_back(far, same)),
        ("reduce_second", reduce_second),
        ("pass_01", lambda: pass_on(*range(min(2, H)))),
        ("sibling_far", lambda: sibling_here(1)),
        ("back_far_other", lambda: multiply_back(far, (1 - r,))),
        ("back_states", back_states),
        ("pass_2", lambda: pass_on(2) if H > 2 else None),
        ("pass_3", lambda: pass_on(3) if H > 3 else None),
        ("reduce2a", lambda: reduce_step(2, 0)),
        ("correlate", lambda: convolve(cgr, False, mix)),
        ("reduce2b", lambda: reduce_step(2, 1)),
        ("pass_last", lambda: pass_on(H)),
        ("gather2_wait1", lambda: gather_wait(1)),
        ("gather2_send2", lambda: gather_send(2)),
        ("send_back_rows", lambda: send_rows(1)),
        ("hand_own", hand_own),
        ("reduce3a", lambda: reduce_step(3, 0)),
        ("reduce3b", lambda: reduce_step(3, 1)),
        ("hand_over", hand_over),
        ("wait_back_rows", lambda: wait_rows(1)),
        ("key_value", key_value),
        ("handed_own", lambda: handed(True)),
        ("gather2_wait2", lambda: gather_wait(2)),
        ("weight_own", lambda: weight_product(own_rows, True)),
        ("mixed_done", mixed_done),
        ("handed_over", lambda: handed(False)),
        ("weight_other", lambda: weight_product(other_rows, False)),
        ("drain", drain),
    ]
    for name, step in steps:
        step()


def transforms(R):
    angle = np.pi / (2 * R) * (np.outer(2 * np.arange(R) + 1, np.arange(R)) % (4 * R))
    there = np.concatenate([np.cos(angle), -np.sin(angle)])
    result = []
    for table in (there, there.T / R):
        high = table.astype(np.float32).astype(ml_dtypes.bfloat16)
        low = (table - high.astype(np.float64)).astype(ml_dtypes.bfloat16)
        result.append(jnp.asarray(np.concatenate([high, low, high], axis=1)))
    return result


def finish(*refs):
    count = len(refs) // 2
    given, made, sem = refs[:count], refs[count : 2 * count], refs[-1]
    copies = [pltpu.make_async_copy(a, b, sem.at[n]) for n, (a, b) in enumerate(zip(given, made))]
    for one in copies:
        one.start()
    for one in copies:
        one.wait()


def solution(mesh):
    N = mesh.shape["context"]
    X = math.isqrt(N)
    Y = N // X
    Z = mesh.shape["tensor"] // 2
    H = Z // 2

    def shards(query_rows, key_rows, value_rows, residue, decay_rate, out_weight, cotangent):
        R, C = query_rows.shape
        M = residue.shape[0]
        small = jax.ShapeDtypeStruct((R, C), BF16)
        dma = pltpu.SemaphoreType.DMA
        top = max(X // 2, Y // 2)
        anywhere = pl.BlockSpec(memory_space=pl.ANY)
        results = (small, small, small, small, jax.ShapeDtypeStruct((C, C), BF16))
        made = pl.pallas_call(
            functools.partial(body, X, Y, Z),
            out_shape=tuple(pltpu.VMEM(one.shape, BF16) for one in results),
            in_specs=[anywhere] * 9,
            out_specs=(pl.BlockSpec(memory_space=pltpu.VMEM),) * 5,
            scratch_shapes=[
                pltpu.VMEM((2 * Z, C, C), BF16),
                pltpu.VMEM((2 * Z, R, C), BF16),
                pltpu.VMEM((N, R, C), BF16),
                pltpu.VMEM((X, Y, R, C), BF16),
                pltpu.VMEM((2 * Z, R, C), BF16),
                pltpu.VMEM((Z, R, C), BF16),
                pltpu.VMEM((2, H, R, C), BF16),
                pltpu.VMEM((2, H, R, C), BF16),
                pltpu.VMEM((2, Y, M, C), F32),
                pltpu.VMEM((2, X, M, C), F32),
                pltpu.VMEM((R, C), BF16),
                pltpu.VMEM((R, C), BF16),
                pltpu.VMEM((R, C), BF16),
                pltpu.VMEM((M, C), F32),
                pltpu.VMEM((M, C), F32),
                pltpu.VMEM((2 * R, 3 * R), BF16),
                pltpu.VMEM((R, 6 * R), BF16),
                dma((8,)),
                pltpu.VMEM((R, C), F32),
                pltpu.VMEM((R, C), F32),
                pltpu.VMEM((R, C), F32),
                pltpu.VMEM((R, C), F32),
                pltpu.VMEM((R, C), F32),
                pltpu.VMEM((R, C), F32),
                pltpu.VMEM((2 * R, C), F32),
                pltpu.VMEM((C, C), F32),
                pltpu.VMEM((M, 8, C), F32),
                pltpu.VMEM((M, 8, C), F32),
                pltpu.VMEM((M, 8, C), F32),
                pltpu.VMEM((M, 8, C), F32),
                dma((1,)),
                dma((1,)),
                dma((2, H, 2)),
                dma((1,)),
                dma((2,)),
                dma((1,)),
                dma((X,)),
                dma((1,)),
                dma((2,)),
                dma((1,)),
                dma((2, X)),
                dma((2,)),
                dma((2,)),
                dma((2,)),
                dma((2,)),
                dma((1,)),
                dma((1,)),
                dma((top,)),
                dma((1,)),
                dma((Z,)),
                dma((1,)),
                dma((2, H, 2)),
            ],
            compiler_params=pltpu.CompilerParams(
                collective_id=0, has_side_effects=True, vmem_limit_bytes=56 * 1024 * 1024
            ),
            name="hyena_block",
        )(query_rows, key_rows, value_rows, residue, decay_rate, out_weight, cotangent, *transforms(R))
        return pl.pallas_call(
            finish,
            out_shape=results,
            in_specs=[anywhere] * 5,
            out_specs=(anywhere,) * 5,
            scratch_shapes=[dma((5,))],
            compiler_params=pltpu.CompilerParams(vmem_limit_bytes=1024 * 1024),
            name="hand_out",
        )(*made)

    placed = (
        P("context", "tensor"),
        P("context", "tensor"),
        P("context", "tensor"),
        P(None, "tensor"),
        P(None, "tensor"),
        P("tensor", None),
        P("context", "tensor"),
    )
    return jax.shard_map(
        shards,
        mesh=mesh,
        in_specs=placed,
        out_specs=(
            P("context", "tensor"),
            P("context", "tensor"),
            P("context", "tensor"),
            P("context", "tensor"),
            P("tensor", "context"),
        ),
        check_vma=False,
    )
```

```python
import functools
import math

import jax
import jax.numpy as jnp
import ml_dtypes
import numpy as np
from jax import lax
from jax.experimental import pallas as pl
from jax.experimental.pallas import tpu as pltpu
from jax.sharding import PartitionSpec as P

MESH = pl.DeviceIdType.MESH
F32 = jnp.float32
BF16 = jnp.bfloat16
LANES = 128


def body(
    X, Y, Z,
    q_in, k_in, v_in, res_in, dec_in, w_ref, cot_in, fold_in, unfold_in,
    mixed_ref, qg_ref, kg_ref, vg_ref, wg_ref,
    wv, cot_all, cot_t, gat, part, sib, rs_out, rs_in, states, row_states,
    q_ref, k_ref, v_ref, res_ref, dec_ref, fold, unfold, in_sem,
    src, cgr, conv, back, mix, taps, taps_hat, wacc, rates, weights, powers, starts,
    w_sem, ag_ss, ag_rs, cs_ss, cs_rs, aa_ss, aa_rs, fw_ss, fw_rs, ex_ss, ex_rs, st_ss, st_rs, ro_ss, ro_rs,
    ga_ss, g1_rs, g2_rs, sb_ss, sb_rs, rr_ss, rr_rs,
):
    N = X * Y
    R, C = q_in.shape
    M = dec_in.shape[0]
    T = R // 8
    G = C // LANES
    H = Z // 2
    c = lax.axis_index("context")
    j = lax.axis_index("tensor")
    z, r = j // 2, j % 2
    cx, cy = c // Y, c % Y
    other = z * 2 + 1 - r
    mine = (c, j)
    sibling = (c, other)
    zdev = [(c, ((z + 1) % Z) * 2 + r), (c, ((z + Z - 1) % Z) * 2 + r)]
    xdev = [(((cx + 1) % X) * Y + cy, j), (((cx + X - 1) % X) * Y + cy, j)]
    ydev = [(cx * Y + (cy + 1) % Y, j), (cx * Y + (cy + Y - 1) % Y, j)]

    def copy(source, target, send_sem, recv_sem, device):
        return pltpu.make_async_remote_copy(
            src_ref=source, dst_ref=target, send_sem=send_sem, recv_sem=recv_sem,
            device_id=device, device_id_type=MESH,
        )

    def arrived(sem, ref):
        copy(ref, ref, sem, sem, mine).wait_recv()

    def left(sem, ref):
        copy(ref, ref, sem, sem, mine).wait_send()

    def lanes_of(g):
        return pl.ds(pl.multiple_of(g * LANES, LANES), LANES)

    barrier = pltpu.get_barrier_semaphore()
    for device in zdev + [sibling]:
        pl.semaphore_signal(barrier, inc=1, device_id=device, device_id_type=MESH)

    @pl.loop(0, N)
    def _(p):
        @pl.when(p != c)
        def _():
            pl.semaphore_signal(barrier, inc=1, device_id=(p, j), device_id_type=MESH)

    loads = (
        (k_in, k_ref), (v_in, v_ref), (dec_in, dec_ref), (cot_in, cot_all.at[j]), (res_in, res_ref),
        (fold_in, fold), (q_in, q_ref), (unfold_in, unfold),
    )

    def load(n):
        return pltpu.make_async_copy(*loads[n], in_sem.at[n])

    for n in range(len(loads)):
        load(n).start()

    def w_copy(n):
        return pltpu.make_async_copy(
            w_ref.at[:, pl.ds(pl.multiple_of(n * C, LANES), C)], wv.at[n], w_sem.at[0]
        )

    @pl.loop(0, 2 * Z)
    def _(n):
        w_copy(n).start()

    rows8 = lax.broadcasted_iota(jnp.int32, (8, LANES), 0).astype(F32)

    def spread_weights():
        load(4).wait()
        weight = res_ref[...] * jnp.sqrt(dec_ref[...])
        for m in range(M):
            weights[m] = jnp.broadcast_to(weight[m : m + 1], (8, C))

    def spread_rates():
        for m in range(M):
            rate = jnp.broadcast_to(dec_ref[pl.ds(m, 1), :], (8, C))
            rates[m] = rate
            powers[m] = jnp.exp(-8.0 * rate)

    def local_states(values, forward):
        way = 0 if forward else 1

        @pl.loop(0, G)
        def _(g):
            lanes = lanes_of(g)
            tiles = [values[pl.ds(8 * a, 8), lanes] for a in range(T)]
            if not forward:
                tiles = tiles[::-1]

            @pl.loop(0, M // 8)
            def _(eight):
                sums = []
                for inner in range(8):
                    m = eight * 8 + inner
                    step = powers[m, :, lanes]
                    total = tiles[0]
                    for tile in tiles[1:]:
                        total = total * step + tile
                    reach = 7.0 - rows8 if forward else rows8
                    total = total * jnp.exp(-rates[m, :, lanes] * reach)
                    sums.append(jnp.sum(total, axis=0, keepdims=True))
                modes = pl.ds(pl.multiple_of(eight * 8, 8), 8)
                states[way, cy, modes, lanes] = jnp.concatenate(sums, axis=0)

    def filter_taps():
        @pl.loop(0, G)
        def _(g):
            lanes = lanes_of(g)

            def add_mode(m, tiles):
                step = powers[m, :, lanes]
                term = weights[m, :, lanes] * jnp.exp(-rates[m, :, lanes] * rows8)
                new = []
                for a in range(T):
                    new.append(tiles[a] + term)
                    term = term * step
                return tuple(new)

            zero = jnp.zeros((8, LANES), F32)
            tiles = lax.fori_loop(0, M, add_mode, (zero,) * T, unroll=4)
            for a in range(T):
                taps[pl.ds(8 * a, 8), lanes] = tiles[a]

    width = min(C, 256)

    def halves(value):
        high = value.astype(BF16)
        return high, (value - high.astype(F32)).astype(BF16)

    def analyse(value):
        high, low = halves(value)
        return jnp.dot(fold[...], jnp.concatenate([high, high, low]), preferred_element_type=F32)

    def filter_spectrum():
        for lo in range(0, C, width):
            lanes = slice(lo, lo + width)
            taps_hat[:, lanes] = analyse(taps[:, lanes])

    def convolve(values, forward, out):
        for lo in range(0, C, width):
            lanes = slice(lo, lo + width)
            both = analyse(values[:, lanes])
            real, imag = both[:R], both[R:]
            tap_real, tap_imag = taps_hat[:R, lanes], taps_hat[R:, lanes]
            if forward:
                new_real = tap_real * real - tap_imag * imag
                new_imag = tap_real * imag + tap_imag * real
            else:
                new_real = tap_real * real + tap_imag * imag
                new_imag = tap_real * imag - tap_imag * real
            real_high, real_low = halves(new_real)
            imag_high, imag_low = halves(new_imag)
            out[:, lanes] = jnp.dot(
                unfold[...],
                jnp.concatenate([real_high, imag_high, real_high, imag_high, real_low, imag_low]),
                preferred_element_type=F32,
            )

    def carry_in(forward):
        way = 0 if forward else 1
        decay = jnp.exp(-float(R) * dec_ref[...])
        row_decay = jnp.exp(-float(R * Y) * dec_ref[...])

        def add_row(n, total):
            return total * row_decay + row_states[way, n if forward else X - 1 - n]

        def add_block(n, total):
            return total * decay + states[way, n if forward else Y - 1 - n]

        total = lax.fori_loop(0, cx if forward else X - 1 - cx, add_row, jnp.zeros((M, C), F32))
        total = lax.fori_loop(0, cy if forward else Y - 1 - cy, add_block, total)
        for m in range(M):
            starts[m] = weights[m] * total[m : m + 1]

    def add_carry(forward, out):
        @pl.loop(0, G)
        def _(g):
            lanes = lanes_of(g)

            def add_mode(m, tiles):
                rate, step = rates[m, :, lanes], powers[m, :, lanes]
                term = starts[m, :, lanes] * jnp.exp(-rate * ((rows8 + 1.0) if forward else (8.0 - rows8)))
                new = []
                for a in range(T):
                    new.append(tiles[a] + term)
                    term = term * step
                return tuple(new)

            order = list(range(T)) if forward else list(range(T))[::-1]
            tiles = lax.fori_loop(
                0, M, add_mode, tuple(out[pl.ds(8 * a, 8), lanes] for a in order), unroll=4
            )
            for n, a in enumerate(order):
                out[pl.ds(8 * a, 8), lanes] = tiles[n]

    def state_copy(way, y, sending):
        ref = states.at[way, cy if sending else y]
        sem = st_rs.at[way]
        return copy(ref, ref, st_ss.at[way], sem, (cx * Y + y, j))

    def row_copy(way, x, sending):
        ref = row_states.at[way, cx if sending else x]
        sem = ro_rs.at[way]
        return copy(ref, ref, ro_ss.at[way], sem, (x * Y + cy, j))

    def others(count, here, act):
        @pl.loop(0, count)
        def _(n):
            pl.when(n != here)(lambda: act(n))

    def send_states(way):
        others(Y, cy, lambda y: state_copy(way, y, True).start())

    def send_rows(way):
        arrived(st_rs.at[way], states.at[way, pl.ds(0, Y - 1)])
        decay = jnp.exp(-float(R) * dec_ref[...])
        order = range(Y) if way == 0 else range(Y)[::-1]
        total = states[way, order[0]]
        for y in order[1:]:
            total = total * decay + states[way, y]
        row_states[way, cx] = total

        others(X, cx, lambda x: row_copy(way, x, True).start())

    def wait_rows(way):
        arrived(ro_rs.at[way], row_states.at[way, pl.ds(0, X - 1)])

    def drain_states(way):
        left(st_ss.at[way], states.at[way, pl.ds(0, Y - 1)])
        left(ro_ss.at[way], row_states.at[way, pl.ds(0, X - 1)])

    near = list(range(-min(2, H - 1), min(2, H - 1) + 1))
    far = [away for away in range(-H + 1, H + 1) if away not in near]

    def piece(way, hop, last, size):
        if hop < last:
            return pl.ds(0, size)
        return pl.ds(way * (size // 2), size // 2)

    def ag_copy(way, hop, k, sending):
        away = hop - 1 if sending else hop
        owner = (z - away + Z) % Z if way == 0 else (z + away) % Z
        ref = cot_all.at[owner * 2 + r, pl.ds(k * (R // 2), R // 2)]
        return copy(ref, ref, ag_ss.at[0], ag_rs.at[way, hop - 1, k], zdev[way])

    def ag_pieces(hop):
        return [(way, k) for k in range(2) for way in range(2) if hop < H or way == k]

    def spread(away):
        ref = cot_all.at[(z + Z + away) % Z * 2 + r]
        group = 0 if away in near else 1
        copy(ref, ref, cs_ss.at[0], cs_rs.at[group], sibling).start()

    def sibling_here(group):
        arrived(cs_rs.at[group], cot_all.at[pl.ds(0, len((near, far)[group]))])

    odd = z % 2
    own_rows = pl.ds(pl.multiple_of(odd * (R // 2), R // 2), R // 2)
    other_rows = pl.ds(pl.multiple_of((1 - odd) * (R // 2), R // 2), R // 2)

    def aa_copy(zz):
        owner = zz * 2 + r
        return copy(
            cot_all.at[owner, own_rows], cot_t.at[c, own_rows], aa_ss.at[0], aa_rs.at[cx], (owner, j)
        )

    def scatter(lo, hi):
        count = hi - lo

        @pl.loop(0, count)
        def _(n):
            zz = (z + Z + lo + (c // 2 + n) % count) % Z

            @pl.when(zz * 2 + r != c)
            def _():
                aa_copy(zz).start()

    def ag_start():
        for way, k in ag_pieces(1):
            ag_copy(way, 1, k, True).start()

    def ag_arrive(hop, half_at):
        for way, k in ag_pieces(hop):
            if k == half_at:
                ag_copy(way, hop, k, False).wait_recv()
                if (way, k) in ag_pieces(hop + 1) and hop < H:
                    ag_copy(way, hop + 1, k, True).start()
        if half_at == 1:
            spread(hop)
            if hop < H:
                spread(-hop)

    half = R // 2

    def gather_first():
        for part_at in range(2):
            ref = gat.at[cx, cy, pl.ds(part_at * half, half)]
            for away in range(1, X):
                to = ((cx + away) % X) * Y + cy if part_at == 0 else cx * Y + (cy + away) % Y
                copy(ref, ref, ga_ss.at[0], g1_rs.at[0], (to, j)).start()

    def gather_first_here():
        arrived(g1_rs.at[0], gat.at[0, pl.ds(0, X - 1)])

    def g2_copy(part_at, way, hop, sending):
        size, last, devices, at, many = (
            (Y, Y // 2, ydev, cy, X) if part_at == 0 else (X, X // 2, xdev, cx, Y)
        )
        away = hop - 1 if sending else hop
        owner = (at - away + size) % size if way == 0 else (at + away) % size
        group = piece(way, hop, last, many)
        rows = pl.ds(part_at * half, half)
        ref = gat.at[group, owner, rows] if part_at == 0 else gat.at[owner, group, rows]
        return copy(ref, ref, ga_ss.at[0], g2_rs.at[hop - 1], devices[way])

    def gather_send(hop):
        if hop <= X // 2:
            for part_at in range(2):
                for way in range(2):
                    g2_copy(part_at, way, hop, True).start()

    def gather_wait(hop):
        if hop <= X // 2:
            arrived(g2_rs.at[hop - 1], gat.at[pl.ds(0, 2 if hop < X // 2 else 1)])

    def sb_copy(zz, sending):
        target = zz * 2 + (1 - r if sending else r)
        return copy(part.at[target], sib.at[zz], sb_ss.at[0], sb_rs.at[zz], sibling)

    def project(lo, hi):
        for o in range(lo, hi):
            hop = H - (o + 1) // 2
            zz = (z + Z + hop * (2 * (o % 2) - 1)) % Z
            gated = gat[cx, cy]
            for core in range(2):
                target = zz * 2 + ((1 - r) if core == 0 else r)
                part[target] = jnp.dot(
                    gated, wv[target], preferred_element_type=F32
                ).astype(BF16)
                if core == 0:
                    sb_copy(zz, True).start()

    halves_of = (pl.ds(0, half), pl.ds(half, half))

    def rr_copy(way, step, k):
        return copy(
            rs_out.at[way, step, halves_of[k]], rs_in.at[way, step, halves_of[k]],
            rr_ss.at[0], rr_rs.at[way, step, k], zdev[way],
        )

    def pair_sum(zz, k):
        return part[zz * 2 + r, halves_of[k]].astype(F32) + sib[zz, halves_of[k]].astype(F32)

    def reduce_target(way, step):
        away = H - step
        return (z + away) % Z if way == 0 else (z - away + Z) % Z

    def reduce_piece(way, step, k, arrived):
        total = pair_sum(reduce_target(way, step), k)
        if arrived:
            rr_copy(way, step - 1, k).wait_recv()
            total = total + rs_in[way, step - 1, halves_of[k]].astype(F32)
        rs_out[way, step, halves_of[k]] = total.astype(BF16)
        rr_copy(way, step, k).start()

    def reduce_first():
        sb_copy((z + H) % Z, False).wait_recv()
        for way in range(2):
            reduce_piece(way, 0, way, False)
        if H > 1:
            for way in range(2):
                sb_copy(reduce_target(way, 1), False).wait_recv()
                reduce_piece(way, 1, 1 - way, False)

    def reduce_second():
        if H > 1:
            for way in range(2):
                reduce_piece(way, 1, way, True)

    def reduce_step(step, k):
        if step < H:
            for way in range(2):
                if k == 0:
                    sb_copy(reduce_target(way, step), False).wait_recv()
                reduce_piece(way, step, k, True)

    def reduce_last():
        sb_copy(z, False).wait_recv()
        for k in range(2):
            total = pair_sum(z, k)
            for way in range(2):
                if H > 1 or way == k:
                    rr_copy(way, H - 1, k).wait_recv()
                    total = total + rs_in[way, H - 1, halves_of[k]].astype(F32)
            mixed_ref[halves_of[k]] = total.astype(BF16)

    active = c % 2 == r

    def fw_copy(own, n):
        ref = cot_t.at[pl.ds(n * Y, Y), own_rows if own else other_rows]
        return copy(ref, ref, fw_ss.at[0], fw_rs.at[0 if own else 1], sibling)

    def ex_copy(way, n, sending):
        side = odd if sending else 1 - odd
        low = pl.multiple_of(side * (R // 2) + way * (R // 4), R // 4)
        ref = cot_t.at[pl.ds(n * Y, Y), pl.ds(low, R // 4)]
        return copy(ref, ref, ex_ss.at[0], ex_rs.at[way, n], zdev[way])

    def group_arrived(n):
        def some(count):
            return lambda: arrived(aa_rs.at[n], cot_t.at[pl.ds(0, count), pl.ds(0, R // 2)])

        pl.when(n == cx)(some(Y - 1))
        pl.when(n != cx)(some(Y))

    def pass_group(n):
        group_arrived(n)
        for way in range(2):
            ex_copy(way, n, True).start()

    reach = (z - c // 2 + Z) % Z

    def pass_on(*distances):
        chosen = [reach == away % Z for away in set(distances) | {-away for away in distances}]

        @pl.when(jnp.logical_and(active, functools.reduce(jnp.logical_or, chosen)))
        def _():
            cot_t[c, own_rows] = cot_all[c, own_rows]
            pl.loop(0, X)(pass_group)

    def hand_own():
        @pl.when(active)
        def _():
            for n in range(X):
                fw_copy(True, n).start()

    def hand_group(n):
        for way in range(2):
            ex_copy(way, n, False).wait_recv()
        fw_copy(False, n).start()

    def hand_over():
        pl.when(active)(lambda: pl.loop(0, X)(hand_group))

    def handed(own):
        rows = pl.ds(0, R // 2)
        pl.when(jnp.logical_not(active))(lambda: arrived(fw_rs.at[0 if own else 1], cot_t.at[:, rows]))

    def drain_passed():
        @pl.when(active)
        def _():
            left(ex_ss.at[0], cot_t.at[:, pl.ds(0, R // 2)])
            left(fw_ss.at[0], cot_t)
            left(aa_ss.at[0], cot_t.at[pl.ds(0, Z - 1), pl.ds(0, R // 2)])

        @pl.when(jnp.logical_not(active))
        def _():
            left(aa_ss.at[0], cot_t.at[pl.ds(0, Z), pl.ds(0, R // 2)])

    def wait_weights():
        pltpu.make_async_copy(wv, wv, w_sem.at[0]).wait()

    def begin():
        for n in (0, 1, 2):
            load(n).wait()
        src[...] = k_ref[...].astype(F32) * v_ref[...].astype(F32)
        spread_rates()
        local_states(src, True)

    def first_sends():
        load(3).wait()
        send_states(0)
        ag_start()
        spread(0)

    def filter_spectrum_loaded():
        for n in (5, 6, 7):
            load(n).wait()
        filter_spectrum()

    def gate():
        carry_in(True)
        add_carry(True, conv)
        gat[cx, cy] = (q_ref[...].astype(F32) * conv[...]).astype(BF16)
        gather_first()

    def multiply_back(distances, cores, first=False):
        if not distances:
            return
        zs = [(z + Z + away) % Z for away in distances]
        blocks = [zz * 2 + core for zz in zs for core in cores]
        total = lax.dot_general(
            jnp.concatenate([cot_all[n] for n in blocks], axis=1),
            jnp.concatenate([wv[n] for n in blocks], axis=1),
            (((1,), (1,)), ((), ())), preferred_element_type=F32,
        )
        back[...] = total if first else back[...] + total

    def back_states():
        qg_ref[...] = (back[...] * conv[...]).astype(BF16)
        cgr[...] = back[...] * q_ref[...].astype(F32)
        local_states(cgr, False)
        send_states(1)

    def key_value():
        carry_in(False)
        add_carry(False, mix)
        kg_ref[...] = (mix[...] * v_ref[...].astype(F32)).astype(BF16)
        vg_ref[...] = (mix[...] * k_ref[...].astype(F32)).astype(BF16)

    def mixed_done():
        reduce_last()

    def weight_product(rows, first):
        total = lax.dot_general(
            gat[:, :, rows].reshape(N * half, C), cot_t[:, rows].reshape(N * half, C),
            (((0,), (0,)), ((), ())), preferred_element_type=F32,
        )
        if first:
            wacc[...] = total
        else:
            wg_ref[...] = (wacc[...] + total).astype(BF16)

    def drain():
        drain_states(0)
        drain_states(1)
        left(ag_ss.at[0], cot_all.at[pl.ds(0, Z - 1)])
        left(cs_ss.at[0], cot_all.at[pl.ds(0, Z)])
        left(sb_ss.at[0], sib)
        left(rr_ss.at[0], cot_all.at[pl.ds(0, Z - 1)])
        left(ga_ss.at[0], cot_all.at[pl.ds(0, N - 1)])
        drain_passed()

    def arrive(hop, k):
        if hop < H:
            ag_arrive(hop, k)

    assert H <= 4 and X == Y and N == 2 * Z
    def scatter_at(away):
        if away <= H:
            scatter(away, away + 1)
            if away < H:
                scatter(-away, -away + 1)

    def projects(lo, hi):
        return lambda: project(min(lo, Z), min(hi, Z))

    same, both = (r,), (0, 1)
    steps = [
        ("begin", begin),
        ("barrier", lambda: pl.semaphore_wait(barrier, N - 1 + 3)),
        ("first_sends", first_sends),
        ("weights", spread_weights),
        ("taps", filter_taps),
        ("spectrum", filter_spectrum_loaded),
        ("send_rows", lambda: send_rows(0)),
        ("arrive1a", lambda: arrive(1, 0)),
        ("convolve", lambda: convolve(src, True, conv)),
        ("arrive1b", lambda: arrive(1, 1)),
        ("wait_rows", lambda: wait_rows(0)),
        ("gate", gate),
        ("arrive2a", lambda: arrive(2, 0)),
        ("wait_weights", wait_weights),
        ("project_1", projects(0, 3)),
        ("arrive2b", lambda: arrive(2, 1)),
        ("scatter_near", lambda: scatter(near[0], near[-1] + 1)),
        ("project_2", projects(3, 5)),
        ("arrive3a", lambda: arrive(3, 0)),
        ("project_3", projects(5, Z)),
        ("arrive3b", lambda: arrive(3, 1)),
        ("reduce_first", reduce_first),
        ("scatter3", lambda: scatter_at(3) if H > 3 else None),
        ("sibling_near", lambda: sibling_here(0)),
        ("back_near", lambda: multiply_back(near, both, True)),
        ("arrive_last", lambda: (ag_arrive(H, 0), ag_arrive(H, 1))),
        ("scatter_last", lambda: scatter_at(H)),
        ("gather1", gather_first_here),
        ("gather2_send1", lambda: gather_send(1)),
        ("back_far_same", lambda: multiply_back(far, same)),
        ("reduce_second", reduce_second),
        ("pass_01", lambda: pass_on(*range(min(2, H)))),
        ("sibling_far", lambda: sibling_here(1)),
        ("back_far_other", lambda: multiply_back(far, (1 - r,))),
        ("back_states", back_states),
        ("pass_2", lambda: pass_on(2) if H > 2 else None),
        ("pass_3", lambda: pass_on(3) if H > 3 else None),
        ("reduce2a", lambda: reduce_step(2, 0)),
        ("correlate", lambda: convolve(cgr, False, mix)),
        ("reduce2b", lambda: reduce_step(2, 1)),
        ("pass_last", lambda: pass_on(H)),
        ("hand_own", hand_own),
        ("gather2_wait1", lambda: gather_wait(1)),
        ("gather2_send2", lambda: gather_send(2)),
        ("send_back_rows", lambda: send_rows(1)),
        ("reduce3a", lambda: reduce_step(3, 0)),
        ("reduce3b", lambda: reduce_step(3, 1)),
        ("hand_over", hand_over),
        ("wait_back_rows", lambda: wait_rows(1)),
        ("key_value", key_value),
        ("handed_own", lambda: handed(True)),
        ("gather2_wait2", lambda: gather_wait(2)),
        ("weight_own", lambda: weight_product(own_rows, True)),
        ("mixed_done", mixed_done),
        ("handed_over", lambda: handed(False)),
        ("weight_other", lambda: weight_product(other_rows, False)),
        ("drain", drain),
    ]
    for name, step in steps:
        step()


def transforms(R):
    angle = np.pi / (2 * R) * (np.outer(2 * np.arange(R) + 1, np.arange(R)) % (4 * R))
    there = np.concatenate([np.cos(angle), -np.sin(angle)])
    result = []
    for table in (there, there.T / R):
        high = table.astype(np.float32).astype(ml_dtypes.bfloat16)
        low = (table - high.astype(np.float64)).astype(ml_dtypes.bfloat16)
        result.append(jnp.asarray(np.concatenate([high, low, high], axis=1)))
    return result


def finish(*refs):
    count = len(refs) // 2
    given, made, sem = refs[:count], refs[count : 2 * count], refs[-1]
    copies = [pltpu.make_async_copy(a, b, sem.at[n]) for n, (a, b) in enumerate(zip(given, made))]
    for one in copies:
        one.start()
    for one in copies:
        one.wait()


def solution(mesh):
    N = mesh.shape["context"]
    X = math.isqrt(N)
    Y = N // X
    Z = mesh.shape["tensor"] // 2
    H = Z // 2

    def shards(query_rows, key_rows, value_rows, residue, decay_rate, out_weight, cotangent):
        R, C = query_rows.shape
        M = residue.shape[0]
        small = jax.ShapeDtypeStruct((R, C), BF16)
        dma = pltpu.SemaphoreType.DMA
        top = max(X // 2, Y // 2)
        anywhere = pl.BlockSpec(memory_space=pl.ANY)
        results = (small, small, small, small, jax.ShapeDtypeStruct((C, C), BF16))
        made = pl.pallas_call(
            functools.partial(body, X, Y, Z),
            out_shape=tuple(pltpu.VMEM(one.shape, BF16) for one in results),
            in_specs=[anywhere] * 9,
            out_specs=(pl.BlockSpec(memory_space=pltpu.VMEM),) * 5,
            scratch_shapes=[
                pltpu.VMEM((2 * Z, C, C), BF16),
                pltpu.VMEM((2 * Z, R, C), BF16),
                pltpu.VMEM((N, R, C), BF16),
                pltpu.VMEM((X, Y, R, C), BF16),
                pltpu.VMEM((2 * Z, R, C), BF16),
                pltpu.VMEM((Z, R, C), BF16),
                pltpu.VMEM((2, H, R, C), BF16),
                pltpu.VMEM((2, H, R, C), BF16),
                pltpu.VMEM((2, Y, M, C), F32),
                pltpu.VMEM((2, X, M, C), F32),
                pltpu.VMEM((R, C), BF16),
                pltpu.VMEM((R, C), BF16),
                pltpu.VMEM((R, C), BF16),
                pltpu.VMEM((M, C), F32),
                pltpu.VMEM((M, C), F32),
                pltpu.VMEM((2 * R, 3 * R), BF16),
                pltpu.VMEM((R, 6 * R), BF16),
                dma((8,)),
                pltpu.VMEM((R, C), F32),
                pltpu.VMEM((R, C), F32),
                pltpu.VMEM((R, C), F32),
                pltpu.VMEM((R, C), F32),
                pltpu.VMEM((R, C), F32),
                pltpu.VMEM((R, C), F32),
                pltpu.VMEM((2 * R, C), F32),
                pltpu.VMEM((C, C), F32),
                pltpu.VMEM((M, 8, C), F32),
                pltpu.VMEM((M, 8, C), F32),
                pltpu.VMEM((M, 8, C), F32),
                pltpu.VMEM((M, 8, C), F32),
                dma((1,)),
                dma((1,)),
                dma((2, H, 2)),
                dma((1,)),
                dma((2,)),
                dma((1,)),
                dma((X,)),
                dma((1,)),
                dma((2,)),
                dma((1,)),
                dma((2, X)),
                dma((2,)),
                dma((2,)),
                dma((2,)),
                dma((2,)),
                dma((1,)),
                dma((1,)),
                dma((top,)),
                dma((1,)),
                dma((Z,)),
                dma((1,)),
                dma((2, H, 2)),
            ],
            compiler_params=pltpu.CompilerParams(
                collective_id=0, has_side_effects=True, vmem_limit_bytes=56 * 1024 * 1024
            ),
            name="hyena_block",
        )(query_rows, key_rows, value_rows, residue, decay_rate, out_weight, cotangent, *transforms(R))
        return pl.pallas_call(
            finish,
            out_shape=results,
            in_specs=[anywhere] * 5,
            out_specs=(anywhere,) * 5,
            scratch_shapes=[dma((5,))],
            compiler_params=pltpu.CompilerParams(vmem_limit_bytes=1024 * 1024),
            name="hand_out",
        )(*made)

    placed = (
        P("context", "tensor"),
        P("context", "tensor"),
        P("context", "tensor"),
        P(None, "tensor"),
        P(None, "tensor"),
        P("tensor", None),
        P("context", "tensor"),
    )
    return jax.shard_map(
        shards,
        mesh=mesh,
        in_specs=placed,
        out_specs=(
            P("context", "tensor"),
            P("context", "tensor"),
            P("context", "tensor"),
            P("context", "tensor"),
            P("tensor", "context"),
        ),
        check_vma=False,
    )
```
